32 devices in a mesh: outer: 4 (over x, core), inner: 8 (over z, y).
Axes of the slice: x: 2, y: 2, z: 4, core: 2. Of those that a mesh axis runs over, the one named last changes fastest.
Arguments:
- leaf_q: float32 [8192, 128], P(('outer', 'inner')), may hold values from -0.375 to 0.375
- q_cot: float32 [8192, 128], P(('outer', 'inner')), may hold values from -6 to 6
- leaf_tri: float32 [4096, 128], P(('outer', 'inner')), as said below
- node_blocks: bfloat16 [3, 4096, 128], P(None, ('outer', 'inner')), as said below
- node_tri: bfloat16 [3, 4096, 128], P(None, ('outer', 'inner')), as said below
- root_cot: float32 [128, 128], replicated, may hold values from -6 to 6
Outputs:
- mat_grad: float32 [8192, 128], P(('outer', 'inner'))
The draws below stay inside these ranges and needn't reach their ends.
Inputs may be any that keep to these rules, and one draw needn't show every extreme that they name: `leaf_tri`: upper triangular; diagonal between 1 and 3. `node_blocks`: at each level, every leaf holds the block of its own child subtree, and all leaves of one child subtree hold equal blocks. `node_tri`: upper triangular with diagonal between 1 and 3; at each level all leaves of one node hold equal triangles.
All inputs are finite; a program needn't handle non-finite values.
Results may differ from the reference program's by a relative error of at most 0.0003.
Values sent between devices are 32-bit elements; how exact they have to be, the bound alone decides.
A program may use at most 64 MiB of HBM per device.

```python
import math
import jax
import jax.numpy as jnp
from jax import lax

N = 128
BLOCK = 32
ROWS_DEV = 256
ROWS = 8192
N_OUTER = 4
N_INNER = 8
DEVICES = 32


def fan_list_drawn():
    fanins = []
    remain = N_INNER
    while remain > 1:
        factor = min(remain, 4)
        fanins.append(factor)
        remain = remain // factor
    fanins.append(N_OUTER)
    return fanins


def upper_triangle(key, matrix_count):
    diag_key, off_key = jax.random.split(key)
    diagonal = jnp.exp(jax.random.uniform(diag_key, (matrix_count, N), minval=0.0, maxval=math.log(3.0)))
    above = jax.random.normal(off_key, (matrix_count, N, N)) * (0.7 * N ** (-0.5))
    return jnp.triu(above, 1) + diagonal[:, :, None] * jnp.eye(N, dtype=jnp.float32)


def draw_leaf_tri(key, part):
    return upper_triangle(jax.random.fold_in(key, 11), DEVICES).reshape(DEVICES * N, N)


def draw_node_blocks(key, part):
    fanins = fan_list_drawn()
    pieces = []
    stride = 1
    for height in range(len(fanins)):
        block_key = jax.random.fold_in(jax.random.fold_in(key, 23), height)
        shape_here = (DEVICES // stride, N, N)
        matrices = jax.random.normal(block_key, shape_here) * (2.0 * N) ** (-0.5)
        pieces.append(jnp.repeat(matrices, stride, axis=0))
        stride = stride * fanins[height]
    return jnp.stack(pieces).reshape(len(fanins), DEVICES * N, N).astype(jnp.bfloat16)


def draw_node_tri(key, part):
    fanins = fan_list_drawn()
    pieces = []
    stride = 1
    for height in range(len(fanins)):
        node_stride = stride * fanins[height]
        tri_key = jax.random.fold_in(jax.random.fold_in(key, 37), height)
        matrices = upper_triangle(tri_key, DEVICES // node_stride)
        pieces.append(jnp.repeat(matrices, node_stride, axis=0))
        stride = node_stride
    return jnp.stack(pieces).reshape(len(fanins), DEVICES * N, N).astype(jnp.bfloat16)


def block_scale(key, shape, shards, smallest, high):
    def one(position, parts):
        steps = jax.random.uniform(jax.random.fold_in(jax.random.fold_in(key, 6), position), (parts,), jnp.float32, smallest / len(shards), high / len(shards))
        return jnp.repeat(jnp.exp(steps), shape[position] // parts).reshape((-1,) + (1,) * (len(shape) - position - 1))

    factor_of = one(*shards[0])
    for cut in shards[1:]:
        factor_of = factor_of * one(*cut)
    return factor_of


def noise(rng, shape, width, bound, cuts=(), kind=jnp.bfloat16):
    drawn = width * jax.random.normal(rng, shape, jnp.float32)
    if cuts:
        drawn = drawn * block_scale(rng, shape, cuts, -0.22, 0.18)
    return jnp.clip(drawn, -bound, bound).astype(kind)


def setup_inputs(seed: int = 0) -> dict:
    splits = jax.random.split(jax.random.key(seed), 7)
    return {
        "leaf_q": noise(splits[0], (ROWS, N), ROWS_DEV ** -0.5, 0.375, ((0, 32),), jnp.float32),
        "q_cot": noise(splits[1], (ROWS, N), 1.0, 6.0, ((0, 32),), jnp.float32),
        "leaf_tri": draw_leaf_tri(jax.random.fold_in(splits[6], 71), 0),
        "node_blocks": draw_node_blocks(jax.random.fold_in(splits[6], 71), 0),
        "node_tri": draw_node_tri(jax.random.fold_in(splits[6], 71), 0),
        "root_cot": noise(splits[5], (N, N), 1.0, 6.0, (), jnp.float32),
    }


def fan_list():
    fanins = []
    remain = N_INNER
    while remain > 1:
        factor = min(remain, 4)
        fanins.append(factor)
        remain = remain // factor
    fanins.append(N_OUTER)
    return fanins


def matmul(left_side, right_side):
    return jnp.matmul(left_side, right_side, precision=lax.Precision.HIGHEST)


def flip_last(matrix):
    return jnp.swapaxes(matrix, -1, -2)


def mirror_lower(matrix):
    return jnp.tril(matrix) + flip_last(jnp.tril(matrix, -1))


def small_inverse(block):
    order = block.shape[-1]
    diag_vals = jnp.diagonal(block, axis1=-2, axis2=-1)
    eye_small = jnp.eye(order, dtype=jnp.float32)
    nilpotent = -jnp.triu(block, 1) / diag_vals[..., :, None]
    product = eye_small + nilpotent
    power = 2
    while power < order:
        nilpotent = matmul(nilpotent, nilpotent)
        product = matmul(product, eye_small + nilpotent)
        power = power * 2
    return product / diag_vals[..., None, :]


def tri_inverse(triangle):
    order = triangle.shape[-1]
    count = order // BLOCK
    inverses = [small_inverse(triangle[..., k * BLOCK:(k + 1) * BLOCK, k * BLOCK:(k + 1) * BLOCK]) for k in range(count)]
    span = BLOCK
    while len(inverses) > 1:
        joined = []
        for pair in range(len(inverses) // 2):
            start = pair * 2 * span
            upper_inv = inverses[2 * pair]
            lower_inv = inverses[2 * pair + 1]
            corner = triangle[..., start:start + span, start + span:start + 2 * span]
            linked = -matmul(matmul(upper_inv, corner), lower_inv)
            top_rows = jnp.concatenate([upper_inv, linked], axis=-1)
            bottom_rows = jnp.concatenate([jnp.zeros_like(lower_inv), lower_inv], axis=-1)
            joined.append(jnp.concatenate([top_rows, bottom_rows], axis=-2))
        inverses = joined
        span = span * 2
    return inverses[0]


def right_solve(triangle, values):
    return matmul(values, flip_last(tri_inverse(triangle)))


def reference(leaf_q, q_cot, leaf_tri, node_blocks, node_tri, root_cot):
    fanins = fan_list()
    levels_count = len(fanins)
    blocks_all = node_blocks.astype(jnp.float32).reshape(levels_count, DEVICES, N, N)
    tris_all = node_tri.astype(jnp.float32).reshape(levels_count, DEVICES, N, N)
    leaf_rows = leaf_q.reshape(DEVICES, ROWS_DEV, N)
    cot_rows = q_cot.reshape(DEVICES, ROWS_DEV, N)
    leaf_tris = leaf_tri.reshape(DEVICES, N, N)
    leaf_sums = matmul(flip_last(leaf_rows), cot_rows)
    child_sums = [leaf_sums]
    strides = []
    stride = 1
    for height in range(levels_count):
        factor = fanins[height]
        strides.append(stride)
        child_blocks = blocks_all[height, ::stride]
        projected = matmul(flip_last(child_blocks), child_sums[-1])
        child_sums.append(jnp.sum(projected.reshape(-1, factor, N, N), axis=1))
        stride = stride * factor
    upper_path = None
    cot_tri = root_cot[None]
    for height in reversed(range(levels_count)):
        factor = fanins[height]
        stride = strides[height]
        child_blocks = blocks_all[height, ::stride]
        node_tris = tris_all[height, ::stride * factor]
        node_sums = child_sums[height + 1]
        own_sums = child_sums[height]
        if upper_path is None:
            middle = matmul(node_tris, flip_last(cot_tri)) - flip_last(node_sums)
            spread = jnp.repeat(mirror_lower(middle), factor, axis=0)
            right_side = own_sums + matmul(child_blocks, spread)
            upper_path = child_blocks
        else:
            middle = matmul(node_tris, flip_last(cot_tri)) - matmul(upper_path, flip_last(node_sums))
            spread = jnp.repeat(mirror_lower(middle), factor, axis=0)
            path_copies = jnp.repeat(upper_path, factor, axis=0)
            right_side = matmul(own_sums, flip_last(path_copies)) + matmul(child_blocks, spread)
            upper_path = matmul(child_blocks, path_copies)
        node_inverse = jnp.repeat(tri_inverse(node_tris), factor, axis=0)
        cot_tri = matmul(right_side, flip_last(node_inverse))
    leaf_cot = matmul(cot_rows, flip_last(upper_path))
    middle = matmul(leaf_tris, flip_last(cot_tri)) - matmul(upper_path, flip_last(leaf_sums))
    gradient = right_solve(leaf_tris, leaf_cot + matmul(leaf_rows, mirror_lower(middle)))
    return gradient.reshape(DEVICES * ROWS_DEV, N)
```

```python
import functools

import jax
import jax.numpy as jnp
from jax import lax
from jax.experimental import pallas as pl
from jax.experimental.pallas import tpu as pltpu
from jax.sharding import PartitionSpec as P

BLOCK = 32
MESH = pl.DeviceIdType.MESH
F32 = jnp.float32
BF16 = jnp.bfloat16


def split(value):
    high = value.astype(BF16)
    return high, (value - high.astype(F32)).astype(BF16)


def dot(left, right, dims):
    return lax.dot_general(left, right, (dims, ((), ())), preferred_element_type=F32)


def product(left, right, dims=((1,), (0,))):
    left_high, left_low = left
    right_high, right_low = right
    total = dot(left_high, right_high, dims)
    if right_low is not None:
        total = total + dot(left_high, right_low, dims)
    if left_low is not None:
        total = total + dot(left_low, right_high, dims)
    return total


def places(order):
    rows = lax.broadcasted_iota(jnp.int32, (order, order), 0)
    columns = lax.broadcasted_iota(jnp.int32, (order, order), 1)
    return rows, columns


def mirror_lower(matrix, rows, columns):
    below = jnp.where(rows > columns, matrix, 0.0)
    return jnp.where(rows >= columns, matrix, 0.0) + below.T


def block_inverses(triangles, rows, columns):
    inside = (rows // BLOCK == columns // BLOCK) & (rows < columns)
    on_diagonal = rows == columns
    eye = jnp.where(on_diagonal, 1.0, 0.0)
    powers, totals, scales = [], [], []
    for triangle in triangles:
        diagonal = jnp.where(on_diagonal, triangle, 0.0)
        down = jnp.sum(diagonal, axis=1, keepdims=True)
        scales.append(jnp.sum(diagonal, axis=0, keepdims=True))
        nilpotent = jnp.where(inside, -triangle, 0.0) / down
        powers.append(split(nilpotent))
        totals.append(eye + nilpotent)
    power = 2
    while power < BLOCK:
        powers = [split(product(value, value)) for value in powers]
        totals = [total + product(split(total), value) for total, value in zip(totals, powers)]
        power = power * 2
    return [total / scale for total, scale in zip(totals, scales)]


def join_inverses(inverses, triangles, rows, columns):
    order = rows.shape[0]
    span = BLOCK
    while span < order:
        corner = (rows // (2 * span) == columns // (2 * span)) & (rows // span < columns // span)
        joined = []
        for inverse, triangle in zip(inverses, triangles):
            parts = split(inverse)
            link = product(parts, split(jnp.where(corner, triangle, 0.0)))
            joined.append(inverse - product(split(link), parts))
        inverses = joined
        span = span * 2
    return inverses


def fan_list(n_outer, n_inner):
    fanins = []
    remain = n_inner
    while remain > 1:
        fanins.append(min(remain, 4))
        remain = remain // fanins[-1]
    fanins.append(n_outer)
    return fanins


def kernel(
    n_outer, n_inner,
    q_hbm, g_hbm, leaf_hbm, blocks_hbm, tri_hbm, root_hbm, out_ref,
    q_ref, g_ref, leaf_ref, blocks_ref, tri_ref, root_ref,
    part_ref, scatter_ref, lift_ref, land_ref, full_ref,
    in_sem, scatter_send, scatter_recv, lift_send, lift_recv, full_send, full_recv,
):
    fanins = fan_list(n_outer, n_inner)
    levels = len(fanins)
    outer, inner = lax.axis_index("outer"), lax.axis_index("inner")
    order = leaf_ref.shape[1]
    first = fanins[0]
    chunk = order // first

    def digit(level):
        if level == levels - 1:
            return outer
        stride = 1
        for factor in fanins[:level]:
            stride = stride * factor
        return lax.rem(inner // stride, fanins[level])

    def peer(level, step):
        mine = digit(level)
        other = lax.rem(mine + step, fanins[level])
        if level == levels - 1:
            return other, (other, inner)
        stride = 1
        for factor in fanins[:level]:
            stride = stride * factor
        return other, (outer, inner + (other - mine) * stride)

    loads = [
        pltpu.make_async_copy(source, target, in_sem.at[k])
        for k, (source, target) in enumerate(
            [
                (g_hbm, g_ref), (q_hbm, q_ref), (blocks_hbm, blocks_ref),
                (leaf_hbm, leaf_ref), (tri_hbm, tri_ref), (root_hbm, root_ref),
            ]
        )
    ]
    for load in loads:
        load.start()
    barrier = pltpu.get_barrier_semaphore()
    greeted = 0
    for level in range(levels):
        for step in range(1, fanins[level]):
            pl.semaphore_signal(barrier, inc=1, device_id=peer(level, step)[1], device_id_type=MESH)
            greeted += 1

    rows, columns = places(order)
    for load in loads[:3]:
        load.wait()
    blocks = [blocks_ref[level] for level in range(levels)]
    cot_parts = split(g_ref[...])
    row_parts = split(q_ref[...])
    leaf_sum = product(split(g_ref[...].T), row_parts)
    leaf_parts = split(leaf_sum)
    part_ref[...] = product(leaf_parts, (blocks[0], None))
    pl.semaphore_wait(barrier, greeted)

    mine = digit(0)
    own = pl.ds(pl.multiple_of(mine * chunk, chunk), chunk)
    scatters = []
    for step in range(1, first):
        other, device = peer(0, step)
        copy = pltpu.make_async_remote_copy(
            src_ref=part_ref.at[pl.ds(pl.multiple_of(other * chunk, chunk), chunk)],
            dst_ref=scatter_ref.at[step - 1],
            send_sem=scatter_send.at[step - 1],
            recv_sem=scatter_recv.at[step - 1],
            device_id=device,
            device_id_type=MESH,
        )
        copy.start()
        scatters.append(copy)

    def spread(level):
        copies = []
        for step in range(1, first):
            copy = pltpu.make_async_remote_copy(
                src_ref=full_ref.at[level, own],
                dst_ref=full_ref.at[level, own],
                send_sem=full_send.at[level, step - 1],
                recv_sem=full_recv.at[level, step - 1],
                device_id=peer(0, step)[1],
                device_id_type=MESH,
            )
            copy.start()
            copies.append(copy)
        return copies

    def lift(level):
        copies = []
        for step in range(1, fanins[level]):
            copy = pltpu.make_async_remote_copy(
                src_ref=lift_ref.at[level - 1],
                dst_ref=land_ref.at[level - 1, step - 1],
                send_sem=lift_send.at[level - 1, step - 1],
                recv_sem=lift_recv.at[level - 1, step - 1],
                device_id=peer(level, step)[1],
                device_id_type=MESH,
            )
            copy.start()
            copies.append(copy)
        return copies

    for load in loads[3:]:
        load.wait()
    triangles = [leaf_ref[...]] + [tri_ref[level].astype(F32) for level in range(levels)]
    inverses = block_inverses(triangles, rows, columns)

    for copy in scatters:
        copy.wait_recv()
    total = part_ref[own, :]
    for step in range(1, first):
        total = total + scatter_ref[step - 1]
    full_ref[0, own, :] = total

    spreads, lifts = [], []
    late = {}

    def paths_and_inverses():
        late["inverses"] = [split(x) for x in join_inverses(inverses, triangles, rows, columns)]
        path = [None] * levels
        path[levels - 1] = (blocks[levels - 1], None)
        for level in reversed(range(levels - 1)):
            path[level] = split(product((blocks[level], None), path[level + 1]))
        late["path"] = path

    def carries():
        inv, path = late["inverses"], late["path"]
        tri_parts = [split(triangles[0])] + [(tri_ref[level], None) for level in range(levels - 1)]
        ratio = [split(product(tri_parts[level], inv[level + 1])) for level in range(levels)]
        late["ratio"] = ratio
        weight = []
        for level in range(levels):
            through = path[level][0].astype(F32)
            if path[level][1] is not None:
                through = through + path[level][1].astype(F32)
            if level == levels - 1:
                carried = ratio[level][0].astype(F32) + ratio[level][1].astype(F32)
            else:
                carried = product(ratio[level], path[level + 1])
            weight.append(split(carried - through))
        late["weight"] = weight
        late["below"] = product(weight[0], leaf_parts)
        late["cot"] = product(
            cot_parts, split(product(inv[0], path[0])), ((1,), (1,))
        )
        late["top"] = product((tri_ref[levels - 1], None), split(root_ref[...]), ((1,), (1,)))

    work = {1: paths_and_inverses, levels - 1: carries}
    done = set()
    for level in range(1, levels):
        lift_ref[level - 1] = product(split(total), (blocks[level], None))
        lifts.append(lift(level))
        spreads.append(spread(level - 1))
        if level == 1:
            paths_and_inverses()
        if level == levels - 1:
            carries()
        for copy in lifts[-1]:
            copy.wait_recv()
        total = lift_ref[level - 1]
        for step in range(1, fanins[level]):
            total = total + land_ref[level - 1, step - 1]
        full_ref[level, own, :] = total
    spreads.append(spread(levels - 1))

    known = [late["below"]]
    for level in range(levels - 1):
        for copy in spreads[level]:
            copy.wait_recv()
        known.append(product(late["weight"][level + 1], split(full_ref[level])))

    for copy in spreads[levels - 1]:
        copy.wait_recv()
    middle = late["top"] - full_ref[levels - 1]
    for level in reversed(range(levels)):
        mirrored = split(mirror_lower(middle, rows, columns))
        turned = product(mirrored, (blocks[level], None), ((1,), (1,)))
        middle = known[level] + product(late["ratio"][level], split(turned))
    mirrored = split(mirror_lower(middle, rows, columns))
    solved = split(product(mirrored, late["inverses"][0], ((1,), (1,))))
    out_ref[...] = late["cot"] + product(row_parts, solved)

    for copy in scatters:
        copy.wait_send()
    for copies in lifts + spreads:
        for copy in copies:
            copy.wait_send()


def on_device(n_outer, n_inner, leaf_q, q_cot, leaf_tri, node_blocks, node_tri, root_cot):
    fanins = fan_list(n_outer, n_inner)
    levels = len(fanins)
    order = leaf_tri.shape[1]
    chunk = order // fanins[0]
    widest = max(fanins[1:])
    dma = pltpu.SemaphoreType.DMA
    args = (leaf_q, q_cot, leaf_tri, node_blocks, node_tri, root_cot)
    return pl.pallas_call(
        functools.partial(kernel, n_outer, n_inner),
        out_shape=jax.ShapeDtypeStruct(leaf_q.shape, F32),
        in_specs=[pl.BlockSpec(memory_space=pl.ANY)] * len(args),
        out_specs=pl.BlockSpec(memory_space=pltpu.VMEM),
        scratch_shapes=[pltpu.VMEM(arg.shape, arg.dtype) for arg in args]
        + [
            pltpu.VMEM((order, order), F32),
            pltpu.VMEM((fanins[0] - 1, chunk, order), F32),
            pltpu.VMEM((levels - 1, chunk, order), F32),
            pltpu.VMEM((levels - 1, widest - 1, chunk, order), F32),
            pltpu.VMEM((levels, order, order), F32),
            dma((len(args),)),
            dma((fanins[0] - 1,)),
            dma((fanins[0] - 1,)),
            dma((levels - 1, widest - 1)),
            dma((levels - 1, widest - 1)),
            dma((levels, fanins[0] - 1)),
            dma((levels, fanins[0] - 1)),
        ],
        compiler_params=pltpu.CompilerParams(
            collective_id=0, has_side_effects=True, vmem_limit_bytes=32 * 2**20
        ),
    )(*args)


def solution(mesh):
    return jax.shard_map(
        functools.partial(on_device, mesh.shape["outer"], mesh.shape["inner"]),
        mesh=mesh,
        in_specs=(
            P(("outer", "inner"), None),
            P(("outer", "inner"), None),
            P(("outer", "inner"), None),
            P(None, ("outer", "inner"), None),
            P(None, ("outer", "inner"), None),
            P(),
        ),
        out_specs=P(("outer", "inner"), None),
        check_vma=False,
    )
```

```python
import functools

import jax
import jax.numpy as jnp
from jax import lax
from jax.experimental import pallas as pl
from jax.experimental.pallas import tpu as pltpu
from jax.sharding import PartitionSpec as P

BLOCK = 32
MESH = pl.DeviceIdType.MESH
F32 = jnp.float32
BF16 = jnp.bfloat16


def split(value):
    high = value.astype(BF16)
    return high, (value - high.astype(F32)).astype(BF16)


def product(left, right, turn_right=False):
    left_high, left_low = left
    right_high, right_low = right
    width = right_high.shape[0 if turn_right else 1]
    along, across = (1, 0) if turn_right else (0, 1)
    wide = right_high
    if right_low is not None:
        wide = jnp.concatenate([right_high, right_low], axis=across)
    if left_low is not None:
        wide = jnp.concatenate([wide, wide], axis=along)
        left_high = jnp.concatenate([left_high, left_low], axis=1)
    total = lax.dot_general(
        left_high, wide, (((1,), (along,)), ((), ())), preferred_element_type=F32
    )
    if right_low is not None:
        total = total[:, :width] + total[:, width:]
    return total


def places(order):
    rows = lax.broadcasted_iota(jnp.int32, (order, order), 0)
    columns = lax.broadcasted_iota(jnp.int32, (order, order), 1)
    return rows, columns


def mirror_lower(matrix, rows, columns):
    below = jnp.where(rows > columns, matrix, 0.0)
    return jnp.where(rows >= columns, matrix, 0.0) + below.T


def block_inverses(triangles, rows, columns):
    inside = (rows // BLOCK == columns // BLOCK) & (rows < columns)
    on_diagonal = rows == columns
    eye = jnp.where(on_diagonal, 1.0, 0.0)
    order = rows.shape[0]
    stacks, scales = [], []
    for triangle in triangles:
        diagonal = jnp.where(on_diagonal, triangle, 0.0)
        down = jnp.sum(diagonal, axis=1, keepdims=True)
        scales.append(jnp.sum(diagonal, axis=0, keepdims=True))
        nilpotent = jnp.where(inside, -triangle, 0.0) / down
        stacks.append((nilpotent, eye + nilpotent))
    power = 2
    while power < BLOCK:
        following = []
        for nilpotent, total in stacks:
            parts = split(nilpotent)
            if power == 2:
                square = product(parts, parts)
                following.append((square, total))
                continue
            both = product(split(jnp.concatenate([nilpotent, total], axis=0)), parts)
            following.append((both[:order], total + both[order:]))
        stacks = following
        power = power * 2
    totals = [total + product(split(total), split(nilpotent)) for nilpotent, total in stacks]
    return [total / scale for total, scale in zip(totals, scales)]


def join_inverses(inverses, triangles, rows, columns):
    order = rows.shape[0]
    span = BLOCK
    while span < order:
        corner = (rows // (2 * span) == columns // (2 * span)) & (rows // span < columns // span)
        joined = []
        for inverse, triangle in zip(inverses, triangles):
            parts = split(inverse)
            link = product(parts, split(jnp.where(corner, triangle, 0.0)))
            joined.append(inverse - product(split(link), parts))
        inverses = joined
        span = span * 2
    return inverses


def fan_list(n_outer, n_inner):
    fanins = []
    remain = n_inner
    while remain > 1:
        fanins.append(min(remain, 4))
        remain = remain // fanins[-1]
    fanins.append(n_outer)
    return fanins


def kernel(
    n_outer, n_inner,
    q_hbm, g_hbm, leaf_hbm, blocks_hbm, tri_hbm, root_hbm, out_ref,
    q_ref, g_ref, leaf_ref, blocks_ref, tri_ref, root_ref,
    part_ref, scatter_ref, lift_ref, land_ref, full_ref,
    in_sem, scatter_send, scatter_recv, lift_send, lift_recv, full_send, full_recv,
):
    fanins = fan_list(n_outer, n_inner)
    levels = len(fanins)
    outer, inner = lax.axis_index("outer"), lax.axis_index("inner")
    order = leaf_ref.shape[1]
    first = fanins[0]
    chunk = order // first

    def digit(level):
        if level == levels - 1:
            return outer
        stride = 1
        for factor in fanins[:level]:
            stride = stride * factor
        return lax.rem(inner // stride, fanins[level])

    def peer(level, step):
        mine = digit(level)
        other = lax.rem(mine + step, fanins[level])
        if level == levels - 1:
            return other, (other, inner)
        stride = 1
        for factor in fanins[:level]:
            stride = stride * factor
        return other, (outer, inner + (other - mine) * stride)

    loads = [
        pltpu.make_async_copy(source, target, in_sem.at[k])
        for k, (source, target) in enumerate(
            [
                (g_hbm, g_ref), (q_hbm, q_ref), (blocks_hbm, blocks_ref),
                (leaf_hbm, leaf_ref), (tri_hbm, tri_ref), (root_hbm, root_ref),
            ]
        )
    ]
    for load in loads:
        load.start()
    barrier = pltpu.get_barrier_semaphore()
    greeted = 0
    for level in range(levels):
        for step in range(1, fanins[level]):
            pl.semaphore_signal(barrier, inc=1, device_id=peer(level, step)[1], device_id_type=MESH)
            greeted += 1

    rows, columns = places(order)
    for load in loads[:3]:
        load.wait()
    blocks = [blocks_ref[level] for level in range(levels)]
    cot_parts = split(g_ref[...])
    row_parts = split(q_ref[...])
    leaf_sum = product(split(g_ref[...].T), row_parts)
    leaf_parts = split(leaf_sum)
    part_ref[...] = product(leaf_parts, (blocks[0], None))
    pl.semaphore_wait(barrier, greeted)

    mine = digit(0)
    own = pl.ds(pl.multiple_of(mine * chunk, chunk), chunk)
    scatters = []
    for step in range(1, first):
        other, device = peer(0, step)
        copy = pltpu.make_async_remote_copy(
            src_ref=part_ref.at[pl.ds(pl.multiple_of(other * chunk, chunk), chunk)],
            dst_ref=scatter_ref.at[step - 1],
            send_sem=scatter_send.at[step - 1],
            recv_sem=scatter_recv.at[step - 1],
            device_id=device,
            device_id_type=MESH,
        )
        copy.start()
        scatters.append(copy)

    def spread(level):
        copies = []
        for step in range(1, first):
            copy = pltpu.make_async_remote_copy(
                src_ref=full_ref.at[level, own],
                dst_ref=full_ref.at[level, own],
                send_sem=full_send.at[level, step - 1],
                recv_sem=full_recv.at[level, step - 1],
                device_id=peer(0, step)[1],
                device_id_type=MESH,
            )
            copy.start()
            copies.append(copy)
        return copies

    def lift(level):
        copies = []
        for step in range(1, fanins[level]):
            copy = pltpu.make_async_remote_copy(
                src_ref=lift_ref.at[level - 1],
                dst_ref=land_ref.at[level - 1, step - 1],
                send_sem=lift_send.at[level - 1, step - 1],
                recv_sem=lift_recv.at[level - 1, step - 1],
                device_id=peer(level, step)[1],
                device_id_type=MESH,
            )
            copy.start()
            copies.append(copy)
        return copies

    for load in loads[3:]:
        load.wait()
    triangles = [leaf_ref[...]] + [tri_ref[level].astype(F32) for level in range(levels)]
    inverses = block_inverses(triangles, rows, columns)

    for copy in scatters:
        copy.wait_recv()
    total = part_ref[own, :]
    for step in range(1, first):
        total = total + scatter_ref[step - 1]
    full_ref[0, own, :] = total

    spreads, lifts = [], []
    late = {}

    def paths_and_inverses():
        late["inverses"] = [split(x) for x in join_inverses(inverses, triangles, rows, columns)]
        path = [None] * levels
        path[levels - 1] = (blocks[levels - 1], None)
        for level in reversed(range(levels - 1)):
            path[level] = split(product((blocks[level], None), path[level + 1]))
        late["path"] = path

    def carries():
        inv, path = late["inverses"], late["path"]
        tri_parts = [split(triangles[0])] + [(tri_ref[level], None) for level in range(levels - 1)]
        ratio = [split(product(tri_parts[level], inv[level + 1])) for level in range(levels)]
        late["ratio"] = ratio
        weight = []
        for level in range(levels):
            through = path[level][0].astype(F32)
            if path[level][1] is not None:
                through = through + path[level][1].astype(F32)
            if level == levels - 1:
                carried = ratio[level][0].astype(F32) + ratio[level][1].astype(F32)
            else:
                carried = product(ratio[level], path[level + 1])
            weight.append(split(carried - through))
        late["weight"] = weight
        late["below"] = product(weight[0], leaf_parts)
        late["cot"] = product(cot_parts, split(product(inv[0], path[0])), True)
        late["top"] = product((tri_ref[levels - 1], None), split(root_ref[...]), True)

    for level in range(1, levels):
        lift_ref[level - 1] = product(split(total), (blocks[level], None))
        lifts.append(lift(level))
        spreads.append(spread(level - 1))
        if level == 1:
            paths_and_inverses()
        if level == levels - 1:
            carries()
        for copy in lifts[-1]:
            copy.wait_recv()
        total = lift_ref[level - 1]
        for step in range(1, fanins[level]):
            total = total + land_ref[level - 1, step - 1]
        full_ref[level, own, :] = total
    spreads.append(spread(levels - 1))

    known = [late["below"]]
    for level in range(levels - 1):
        for copy in spreads[level]:
            copy.wait_recv()
        known.append(product(late["weight"][level + 1], split(full_ref[level])))

    for copy in spreads[levels - 1]:
        copy.wait_recv()
    middle = late["top"] - full_ref[levels - 1]
    for level in reversed(range(levels)):
        mirrored = split(mirror_lower(middle, rows, columns))
        turned = product(mirrored, (blocks[level], None), True)
        middle = known[level] + product(late["ratio"][level], split(turned))
    mirrored = split(mirror_lower(middle, rows, columns))
    solved = split(product(mirrored, late["inverses"][0], True))
    out_ref[...] = late["cot"] + product(row_parts, solved)

    for copy in scatters:
        copy.wait_send()
    for copies in lifts + spreads:
        for copy in copies:
            copy.wait_send()


def on_device(n_outer, n_inner, leaf_q, q_cot, leaf_tri, node_blocks, node_tri, root_cot):
    fanins = fan_list(n_outer, n_inner)
    levels = len(fanins)
    order = leaf_tri.shape[1]
    chunk = order // fanins[0]
    widest = max(fanins[1:])
    dma = pltpu.SemaphoreType.DMA
    args = (leaf_q, q_cot, leaf_tri, node_blocks, node_tri, root_cot)
    return pl.pallas_call(
        functools.partial(kernel, n_outer, n_inner),
        out_shape=jax.ShapeDtypeStruct(leaf_q.shape, F32),
        in_specs=[pl.BlockSpec(memory_space=pltpu.HBM)] * len(args),
        out_specs=pl.BlockSpec(memory_space=pltpu.VMEM),
        scratch_shapes=[pltpu.VMEM(arg.shape, arg.dtype) for arg in args]
        + [
            pltpu.VMEM((order, order), F32),
            pltpu.VMEM((fanins[0] - 1, chunk, order), F32),
            pltpu.VMEM((levels - 1, chunk, order), F32),
            pltpu.VMEM((levels - 1, widest - 1, chunk, order), F32),
            pltpu.VMEM((levels, order, order), F32),
            dma((len(args),)),
            dma((fanins[0] - 1,)),
            dma((fanins[0] - 1,)),
            dma((levels - 1, widest - 1)),
            dma((levels - 1, widest - 1)),
            dma((levels, fanins[0] - 1)),
            dma((levels, fanins[0] - 1)),
        ],
        compiler_params=pltpu.CompilerParams(
            collective_id=0, has_side_effects=True, vmem_limit_bytes=60 * 2**20
        ),
    )(*args)


def solution(mesh):
    return jax.shard_map(
        functools.partial(on_device, mesh.shape["outer"], mesh.shape["inner"]),
        mesh=mesh,
        in_specs=(
            P(("outer", "inner"), None),
            P(("outer", "inner"), None),
            P(("outer", "inner"), None),
            P(None, ("outer", "inner"), None),
            P(None, ("outer", "inner"), None),
            P(),
        ),
        out_specs=P(("outer", "inner"), None),
        check_vma=False,
    )
```

```python
import functools

import jax
import jax.numpy as jnp
from jax import lax
from jax.experimental import pallas as pl
from jax.experimental.pallas import tpu as pltpu
from jax.sharding import PartitionSpec as P

BLOCK = 32
MESH = pl.DeviceIdType.MESH
F32 = jnp.float32
BF16 = jnp.bfloat16


def split(value):
    high = value.astype(BF16)
    return high, (value - high.astype(F32)).astype(BF16)


def product(left, right, turn_right=False):
    left_high, left_low = left
    right_high, right_low = right
    width = right_high.shape[0 if turn_right else 1]
    along, across = (1, 0) if turn_right else (0, 1)
    wide = right_high
    if right_low is not None:
        wide = jnp.concatenate([right_high, right_low], axis=across)
    if left_low is not None:
        wide = jnp.concatenate([wide, wide], axis=along)
        left_high = jnp.concatenate([left_high, left_low], axis=1)
    total = lax.dot_general(
        left_high, wide, (((1,), (along,)), ((), ())), preferred_element_type=F32
    )
    if right_low is not None:
        total = total[:, :width] + total[:, width:]
    return total


def places(order):
    rows = lax.broadcasted_iota(jnp.int32, (order, order), 0)
    columns = lax.broadcasted_iota(jnp.int32, (order, order), 1)
    return rows, columns


def mirror_lower(matrix, rows, columns):
    below = jnp.where(rows > columns, matrix, 0.0)
    return jnp.where(rows >= columns, matrix, 0.0) + below.T


def unpack(parts, inside):
    copies = inside.shape[0] // parts[0].shape[0]
    return tuple(jnp.concatenate([part] * copies, axis=0) * inside for part in parts)


def fold(matrix, span):
    total = matrix[:span]
    for start in range(span, matrix.shape[0], span):
        total = total + matrix[start : start + span]
    return total


def block_inverses(triangles, rows, columns):
    same = rows // BLOCK == columns // BLOCK
    inside = jnp.where(same, 1.0, 0.0).astype(BF16)
    on_diagonal = rows == columns
    eye = fold(jnp.where(on_diagonal, 1.0, 0.0), BLOCK)
    stacks, scales = [], []
    for triangle in triangles:
        diagonal = jnp.where(on_diagonal, triangle, 0.0)
        down = jnp.sum(diagonal, axis=1, keepdims=True)
        scales.append(jnp.sum(diagonal, axis=0, keepdims=True))
        nilpotent = fold(jnp.where(same & (rows < columns), -triangle, 0.0) / down, BLOCK)
        stacks.append((nilpotent, eye + nilpotent))
    power = 2
    while power < BLOCK:
        following = []
        for nilpotent, total in stacks:
            parts = split(nilpotent)
            if power == 2:
                following.append((product(parts, unpack(parts, inside)), total))
                continue
            stacked = split(jnp.concatenate([nilpotent, total], axis=0))
            both = product(stacked, unpack(parts, inside))
            following.append((both[:BLOCK], total + both[BLOCK:]))
        stacks = following
        power = power * 2
    return [
        (total + product(split(total), unpack(split(nilpotent), inside))) / scale
        for (nilpotent, total), scale in zip(stacks, scales)
    ]


def join_inverses(inverses, triangle_parts, rows, columns):
    order = rows.shape[0]
    span = BLOCK
    while span < order:
        row_block, column_block = rows // span, columns // span
        corner = (rows // (2 * span) == columns // (2 * span)) & (row_block < column_block)
        corner = jnp.where(corner, 1.0, 0.0).astype(BF16)
        inside = jnp.where(row_block == column_block, 1.0, 0.0).astype(BF16)
        even = lax.rem(column_block[:span], 2) == 0
        joined = []
        for inverse, (high, low) in zip(inverses, triangle_parts):
            edge = (high * corner, None if low is None else low * corner)
            upper = split(jnp.where(even, inverse, 0.0))
            link = product(split(product(upper, edge)), unpack(split(inverse), inside))
            top = jnp.where(even, inverse, -link)
            joined.append(jnp.concatenate([top, jnp.where(even, 0.0, inverse)], axis=0))
        inverses = joined
        span = span * 2
    return inverses


def fan_list(n_outer, n_inner):
    fanins = []
    remain = n_inner
    while remain > 1:
        fanins.append(min(remain, 4))
        remain = remain // fanins[-1]
    fanins.append(n_outer)
    return fanins


def scatter_groups(fanins, order):
    groups = [fanins[0]]
    if len(fanins) > 2 and order % (8 * fanins[0] * fanins[1]) == 0:
        groups.append(fanins[0] * fanins[1])
    return groups


def add_all(terms):
    while len(terms) > 1:
        pairs = [left + right for left, right in zip(terms[::2], terms[1::2])]
        terms = pairs + terms[len(terms) & ~1 :]
    return terms[0]


def kernel(
    n_outer, n_inner,
    q_hbm, g_hbm, leaf_hbm, blocks_hbm, tri_hbm, root_hbm, out_ref,
    q_ref, g_ref, leaf_ref, blocks_ref, tri_ref, root_ref,
    part_ref, scatter_ref, lift_ref, land_ref, full_ref,
    in_sem, scatter_send, scatter_recv, lift_send, lift_recv, full_send, full_recv,
):
    fanins = fan_list(n_outer, n_inner)
    levels = len(fanins)
    groups = scatter_groups(fanins, leaf_ref.shape[1])
    merged = len(groups)
    outer, inner = lax.axis_index("outer"), lax.axis_index("inner")
    order = leaf_ref.shape[1]

    def near(size, step):
        mine = lax.rem(inner, size)
        other = lax.rem(mine + step, size)
        return other, (outer, inner + other - mine)

    def above(level, step):
        if level == levels - 1:
            return (lax.rem(outer + step, n_outer), inner)
        stride = 1
        for factor in fanins[:level]:
            stride = stride * factor
        mine = lax.rem(inner // stride, fanins[level])
        other = lax.rem(mine + step, fanins[level])
        return (outer, inner + (other - mine) * stride)

    def own_rows(size):
        rows_each = order // size
        return pl.ds(pl.multiple_of(lax.rem(inner, size) * rows_each, rows_each), rows_each)

    loads = [
        pltpu.make_async_copy(source, target, in_sem.at[k])
        for k, (source, target) in enumerate(
            [
                (g_hbm, g_ref), (q_hbm, q_ref), (blocks_hbm, blocks_ref),
                (leaf_hbm, leaf_ref), (tri_hbm, tri_ref), (root_hbm, root_ref),
            ]
        )
    ]
    for load in loads:
        load.start()
    barrier = pltpu.get_barrier_semaphore()
    greeted = [near(groups[-1], step)[1] for step in range(1, groups[-1])]
    for level in range(merged, levels):
        greeted += [above(level, step) for step in range(1, fanins[level])]
    for device in greeted:
        pl.semaphore_signal(barrier, inc=1, device_id=device, device_id_type=MESH)

    def send(source, target, send_sem, recv_sem, device):
        copy = pltpu.make_async_remote_copy(
            src_ref=source, dst_ref=target, send_sem=send_sem, recv_sem=recv_sem,
            device_id=device, device_id_type=MESH,
        )
        copy.start()
        return copy

    def scatter(level):
        size = groups[level]
        rows_each = order // size
        copies = []
        for step in range(1, size):
            other, device = near(size, step)
            copies.append(
                send(
                    part_ref.at[level, pl.ds(pl.multiple_of(other * rows_each, rows_each), rows_each)],
                    scatter_ref.at[level, step - 1, pl.ds(0, rows_each)],
                    scatter_send.at[level, step - 1], scatter_recv.at[level, step - 1], device,
                )
            )
        return copies

    def gathered(level, copies):
        size = groups[level]
        for copy in copies:
            copy.wait_recv()
        terms = [part_ref[level, own_rows(size), :]]
        terms += [scatter_ref[level, step, : order // size] for step in range(size - 1)]
        return add_all(terms)

    def lift(level, value):
        slot = level - merged
        lift_ref[slot] = value
        return [
            send(
                lift_ref.at[slot], land_ref.at[slot, step - 1],
                lift_send.at[slot, step - 1], lift_recv.at[slot, step - 1], above(level, step),
            )
            for step in range(1, fanins[level])
        ]

    def spread(level, value):
        size = groups[min(level, merged - 1)]
        own = own_rows(size)
        full_ref[level, own, :] = value
        return [
            send(
                full_ref.at[level, own], full_ref.at[level, own],
                full_send.at[level, step - 1], full_recv.at[level, step - 1], near(size, step)[1],
            )
            for step in range(1, size)
        ]

    rows, columns = places(order)
    for load in loads[:3]:
        load.wait()
    blocks = [blocks_ref[level] for level in range(levels)]
    leaf_sum = product(split(g_ref[...].T), split(q_ref[...]))
    leaf_parts = split(leaf_sum)
    climb = (blocks[0], None)
    part_ref[0] = product(leaf_parts, climb)
    for level in range(1, merged):
        climb = split(product(climb, (blocks[level], None)))
        part_ref[level] = product(leaf_parts, climb)
    pl.semaphore_wait(barrier, len(greeted))
    scatters = [None] * merged
    for level in reversed(range(merged)):
        scatters[level] = scatter(level)

    for load in loads[3:]:
        load.wait()
    triangles = [leaf_ref[...]] + [tri_ref[level].astype(F32) for level in range(levels)]
    triangle_parts = [split(triangles[0])] + [(tri_ref[level], None) for level in range(levels)]
    inverses = block_inverses(triangles, rows, columns)

    lifts, spreads = [], [None] * levels
    total = gathered(merged - 1, scatters[merged - 1])
    for level in range(merged, levels):
        value = product(split(total), (blocks[level], None))
        lifts.append(lift(level, value))
        spreads[level - 1] = spread(level - 1, total)
        if level == merged:
            for below in reversed(range(merged - 1)):
                spreads[below] = spread(below, gathered(below, scatters[below]))
            inverse_parts = [
                split(inverse)
                for inverse in join_inverses(inverses, triangle_parts, rows, columns)
            ]
            path = [None] * levels
            path[levels - 1] = (blocks[levels - 1], None)
            for low in reversed(range(levels - 1)):
                path[low] = split(product((blocks[low], None), path[low + 1]))
            ratio_sums = [
                product(triangle_parts[low], inverse_parts[low + 1]) for low in range(levels)
            ]
            ratio = [split(value) for value in ratio_sums]
        for copy in lifts[-1]:
            copy.wait_recv()
        terms = [lift_ref[level - merged]]
        terms += [land_ref[level - merged, step] for step in range(fanins[level] - 1)]
        total = add_all(terms)
    spreads[levels - 1] = spread(levels - 1, total)

    top = product(triangle_parts[levels], split(root_ref[...]), True)
    known = []
    for level in range(levels):
        through = path[level][0].astype(F32)
        if path[level][1] is not None:
            through = through + path[level][1].astype(F32)
        carried = ratio_sums[level]
        if level < levels - 1:
            carried = product(ratio[level], path[level + 1])
        if level == 0:
            own_sums = leaf_parts
        else:
            for copy in spreads[level - 1]:
                copy.wait_recv()
            own_sums = split(full_ref[level - 1])
        known.append(product(split(carried - through), own_sums))
    cot = product(split(g_ref[...]), split(product(inverse_parts[0], path[0])), True)
    row_parts = split(q_ref[...])

    for copy in spreads[levels - 1]:
        copy.wait_recv()
    middle = top - full_ref[levels - 1]
    for level in reversed(range(levels)):
        mirrored = split(mirror_lower(middle, rows, columns))
        turned = product(mirrored, (blocks[level], None), True)
        middle = known[level] + product(ratio[level], split(turned))
    mirrored = split(mirror_lower(middle, rows, columns))
    solved = split(product(mirrored, inverse_parts[0], True))
    out_ref[...] = cot + product(row_parts, solved)

    for copies in scatters + lifts + spreads:
        for copy in copies:
            copy.wait_send()


def on_device(n_outer, n_inner, leaf_q, q_cot, leaf_tri, node_blocks, node_tri, root_cot):
    fanins = fan_list(n_outer, n_inner)
    levels = len(fanins)
    order = leaf_tri.shape[1]
    groups = scatter_groups(fanins, order)
    merged = len(groups)
    lifted = levels - merged
    widest = max(fanins[merged:]) - 1
    near = groups[-1] - 1
    dma = pltpu.SemaphoreType.DMA
    args = (leaf_q, q_cot, leaf_tri, node_blocks, node_tri, root_cot)
    return pl.pallas_call(
        functools.partial(kernel, n_outer, n_inner),
        out_shape=jax.ShapeDtypeStruct(leaf_q.shape, F32),
        in_specs=[pl.BlockSpec(memory_space=pltpu.HBM)] * len(args),
        out_specs=pl.BlockSpec(memory_space=pltpu.VMEM),
        scratch_shapes=[pltpu.VMEM(arg.shape, arg.dtype) for arg in args]
        + [
            pltpu.VMEM((merged, order, order), F32),
            pltpu.VMEM((merged, near, order // groups[0], order), F32),
            pltpu.VMEM((lifted, order // groups[-1], order), F32),
            pltpu.VMEM((lifted, widest, order // groups[-1], order), F32),
            pltpu.VMEM((levels, order, order), F32),
            dma((len(args),)),
            dma((merged, near)),
            dma((merged, near)),
            dma((lifted, widest)),
            dma((lifted, widest)),
            dma((levels, near)),
            dma((levels, near)),
        ],
        compiler_params=pltpu.CompilerParams(
            collective_id=0, has_side_effects=True, vmem_limit_bytes=60 * 2**20
        ),
    )(*args)


def solution(mesh):
    return jax.shard_map(
        functools.partial(on_device, mesh.shape["outer"], mesh.shape["inner"]),
        mesh=mesh,
        in_specs=(
            P(("outer", "inner"), None),
            P(("outer", "inner"), None),
            P(("outer", "inner"), None),
            P(None, ("outer", "inner"), None),
            P(None, ("outer", "inner"), None),
            P(),
        ),
        out_specs=P(("outer", "inner"), None),
        check_vma=False,
    )
```

```python
import functools

import jax
import jax.numpy as jnp
from jax import lax
from jax.experimental import pallas as pl
from jax.experimental.pallas import tpu as pltpu
from jax.sharding import PartitionSpec as P

BLOCK = 32
MESH = pl.DeviceIdType.MESH
F32 = jnp.float32
BF16 = jnp.bfloat16


def split(value):
    high = value.astype(BF16)
    return high, (value - high.astype(F32)).astype(BF16)


def product(left, right, turn_right=False):
    left_high, left_low = left
    right_high, right_low = right
    width = right_high.shape[0 if turn_right else 1]
    along, across = (1, 0) if turn_right else (0, 1)
    wide = right_high
    if right_low is not None:
        wide = jnp.concatenate([right_high, right_low], axis=across)
    if left_low is not None:
        wide = jnp.concatenate([wide, wide], axis=along)
        left_high = jnp.concatenate([left_high, left_low], axis=1)
    total = lax.dot_general(
        left_high, wide, (((1,), (along,)), ((), ())), preferred_element_type=F32
    )
    if right_low is not None:
        total = total[:, :width] + total[:, width:]
    return total


def places(order):
    rows = lax.broadcasted_iota(jnp.int32, (order, order), 0)
    columns = lax.broadcasted_iota(jnp.int32, (order, order), 1)
    return rows, columns


def mirror_lower(matrix, rows, columns):
    below = jnp.where(rows > columns, matrix, 0.0)
    return jnp.where(rows >= columns, matrix, 0.0) + below.T


def unpack(parts, inside):
    copies = inside.shape[0] // parts[0].shape[0]
    return tuple(jnp.concatenate([part] * copies, axis=0) * inside for part in parts)


def fold(matrix, span):
    total = matrix[:span]
    for start in range(span, matrix.shape[0], span):
        total = total + matrix[start : start + span]
    return total


def block_inverses(triangles, rows, columns):
    same = rows // BLOCK == columns // BLOCK
    inside = jnp.where(same, 1.0, 0.0).astype(BF16)
    on_diagonal = rows == columns
    eye = fold(jnp.where(on_diagonal, 1.0, 0.0), BLOCK)
    stacks, scales = [], []
    for triangle in triangles:
        diagonal = jnp.where(on_diagonal, triangle, 0.0)
        down = jnp.sum(diagonal, axis=1, keepdims=True)
        scales.append(jnp.sum(diagonal, axis=0, keepdims=True))
        nilpotent = fold(jnp.where(same & (rows < columns), -triangle, 0.0) / down, BLOCK)
        stacks.append((nilpotent, eye + nilpotent))
    power = 2
    while power < BLOCK:
        following = []
        for nilpotent, total in stacks:
            parts = split(nilpotent)
            if power == 2:
                following.append((product(parts, unpack(parts, inside)), total))
                continue
            stacked = split(jnp.concatenate([nilpotent, total], axis=0))
            both = product(stacked, unpack(parts, inside))
            following.append((both[:BLOCK], total + both[BLOCK:]))
        stacks = following
        power = power * 2
    return [
        (total + product(split(total), unpack(split(nilpotent), inside))) / scale
        for (nilpotent, total), scale in zip(stacks, scales)
    ]


def join_inverses(inverses, triangle_parts, rows, columns):
    order = rows.shape[0]
    span = BLOCK
    while span < order:
        row_block, column_block = rows // span, columns // span
        corner = (rows // (2 * span) == columns // (2 * span)) & (row_block < column_block)
        corner = jnp.where(corner, 1.0, 0.0).astype(BF16)
        inside = jnp.where(row_block == column_block, 1.0, 0.0).astype(BF16)
        even = lax.rem(column_block[:span], 2) == 0
        joined = []
        for inverse, (high, low) in zip(inverses, triangle_parts):
            edge = (high * corner, None if low is None else low * corner)
            upper = split(jnp.where(even, inverse, 0.0))
            link = product(split(product(upper, edge)), unpack(split(inverse), inside))
            top = jnp.where(even, inverse, -link)
            joined.append(jnp.concatenate([top, jnp.where(even, 0.0, inverse)], axis=0))
        inverses = joined
        span = span * 2
    return inverses


def fan_list(n_outer, n_inner):
    fanins = []
    remain = n_inner
    while remain > 1:
        fanins.append(min(remain, 4))
        remain = remain // fanins[-1]
    fanins.append(n_outer)
    return fanins


def scatter_groups(fanins, order):
    groups = [fanins[0]]
    if len(fanins) > 2 and order % (8 * fanins[0] * fanins[1]) == 0:
        groups.append(fanins[0] * fanins[1])
    return groups


def add_all(terms):
    while len(terms) > 1:
        pairs = [left + right for left, right in zip(terms[::2], terms[1::2])]
        terms = pairs + terms[len(terms) & ~1 :]
    return terms[0]


def kernel(
    n_outer, n_inner,
    q_hbm, g_hbm, leaf_hbm, blocks_hbm, tri_hbm, root_hbm, out_ref,
    q_ref, g_ref, leaf_ref, blocks_ref, tri_ref, root_ref,
    part_ref, scatter_ref, lift_ref, land_ref, full_ref,
    in_sem, scatter_send, scatter_recv, lift_send, lift_recv, full_send, full_recv,
):
    fanins = fan_list(n_outer, n_inner)
    levels = len(fanins)
    groups = scatter_groups(fanins, leaf_ref.shape[1])
    merged = len(groups)
    outer, inner = lax.axis_index("outer"), lax.axis_index("inner")
    order = leaf_ref.shape[1]

    def near(size, step):
        mine = lax.rem(inner, size)
        other = lax.rem(mine + step, size)
        return other, (outer, inner + other - mine)

    def above(level, step):
        if level == levels - 1:
            return (lax.rem(outer + step, n_outer), inner)
        stride = 1
        for factor in fanins[:level]:
            stride = stride * factor
        mine = lax.rem(inner // stride, fanins[level])
        other = lax.rem(mine + step, fanins[level])
        return (outer, inner + (other - mine) * stride)

    def own_rows(size):
        rows_each = order // size
        return pl.ds(pl.multiple_of(lax.rem(inner, size) * rows_each, rows_each), rows_each)

    loads = [
        pltpu.make_async_copy(source, target, in_sem.at[k])
        for k, (source, target) in enumerate(
            [
                (g_hbm, g_ref), (q_hbm, q_ref), (blocks_hbm, blocks_ref),
                (leaf_hbm, leaf_ref), (tri_hbm, tri_ref), (root_hbm, root_ref),
            ]
        )
    ]
    for load in loads:
        load.start()
    barrier = pltpu.get_barrier_semaphore()
    greeted = [near(groups[-1], step)[1] for step in range(1, groups[-1])]
    for level in range(merged, levels):
        greeted += [above(level, step) for step in range(1, fanins[level])]
    for device in greeted:
        pl.semaphore_signal(barrier, inc=1, device_id=device, device_id_type=MESH)

    def send(source, target, send_sem, recv_sem, device):
        copy = pltpu.make_async_remote_copy(
            src_ref=source, dst_ref=target, send_sem=send_sem, recv_sem=recv_sem,
            device_id=device, device_id_type=MESH,
        )
        copy.start()
        return copy

    def scatter(level):
        size = groups[level]
        rows_each = order // size
        copies = []
        for step in range(1, size):
            other, device = near(size, step)
            copies.append(
                send(
                    part_ref.at[level, pl.ds(pl.multiple_of(other * rows_each, rows_each), rows_each)],
                    scatter_ref.at[level, step - 1, pl.ds(0, rows_each)],
                    scatter_send.at[level, step - 1], scatter_recv.at[level, step - 1], device,
                )
            )
        return copies

    def gathered(level, copies):
        size = groups[level]
        for copy in copies:
            copy.wait_recv()
        terms = [part_ref[level, own_rows(size), :]]
        terms += [scatter_ref[level, step, : order // size] for step in range(size - 1)]
        return add_all(terms)

    def lift(level, value):
        slot = level - merged
        lift_ref[slot] = value
        return [
            send(
                lift_ref.at[slot], land_ref.at[slot, step - 1],
                lift_send.at[slot, step - 1], lift_recv.at[slot, step - 1], above(level, step),
            )
            for step in range(1, fanins[level])
        ]

    def spread(level, value):
        size = groups[min(level, merged - 1)]
        own = own_rows(size)
        full_ref[level, own, :] = value
        return [
            send(
                full_ref.at[level, own], full_ref.at[level, own],
                full_send.at[level, step - 1], full_recv.at[level, step - 1], near(size, step)[1],
            )
            for step in range(1, size)
        ]

    rows, columns = places(order)
    for load in loads[:3]:
        load.wait()
    blocks = [blocks_ref[level] for level in range(levels)]
    leaf_sum = product(split(g_ref[...].T), split(q_ref[...]))
    leaf_parts = split(leaf_sum)
    climb = (blocks[0], None)
    part_ref[0] = product(leaf_parts, climb)
    for level in range(1, merged):
        climb = split(product(climb, (blocks[level], None)))
        part_ref[level] = product(leaf_parts, climb)
    pl.semaphore_wait(barrier, len(greeted))
    scatters = [None] * merged
    for level in reversed(range(merged)):
        scatters[level] = scatter(level)

    for load in loads[3:]:
        load.wait()
    triangles = [leaf_ref[...]] + [tri_ref[level].astype(F32) for level in range(levels)]
    triangle_parts = [split(triangles[0])] + [(tri_ref[level], None) for level in range(levels)]
    inverses = block_inverses(triangles, rows, columns)

    lifts, spreads = [], [None] * levels
    total = gathered(merged - 1, scatters[merged - 1])
    for level in range(merged, levels):
        value = product(split(total), (blocks[level], None))
        lifts.append(lift(level, value))
        spreads[level - 1] = spread(level - 1, total)
        if level == merged:
            for below in reversed(range(merged - 1)):
                spreads[below] = spread(below, gathered(below, scatters[below]))
            inverse_parts = [
                split(inverse)
                for inverse in join_inverses(inverses, triangle_parts, rows, columns)
            ]
            path = [None] * levels
            path[levels - 1] = (blocks[levels - 1], None)
            for low in reversed(range(levels - 1)):
                path[low] = split(product((blocks[low], None), path[low + 1]))
            ratio_sums = [
                product(triangle_parts[low], inverse_parts[low + 1]) for low in range(levels)
            ]
            ratio = [split(value) for value in ratio_sums]
        for copy in lifts[-1]:
            copy.wait_recv()
        terms = [lift_ref[level - merged]]
        terms += [land_ref[level - merged, step] for step in range(fanins[level] - 1)]
        total = add_all(terms)
    spreads[levels - 1] = spread(levels - 1, total)

    top = product(triangle_parts[levels], split(root_ref[...]), True)
    known = []
    for level in range(levels):
        through = path[level][0].astype(F32)
        if path[level][1] is not None:
            through = through + path[level][1].astype(F32)
        carried = ratio_sums[level]
        if level < levels - 1:
            carried = product(ratio[level], path[level + 1])
        if level == 0:
            own_sums = leaf_parts
        else:
            for copy in spreads[level - 1]:
                copy.wait_recv()
            own_sums = split(full_ref[level - 1])
        known.append(product(split(carried - through), own_sums))
    cot = product(split(g_ref[...]), split(product(inverse_parts[0], path[0])), True)
    row_parts = split(q_ref[...])

    for copy in spreads[levels - 1]:
        copy.wait_recv()
    middle = top - full_ref[levels - 1]
    for level in reversed(range(levels)):
        mirrored = split(mirror_lower(middle, rows, columns))
        turned = product(mirrored, (blocks[level], None), True)
        middle = known[level] + product(ratio[level], split(turned))
    mirrored = split(mirror_lower(middle, rows, columns))
    solved = split(product(mirrored, inverse_parts[0], True))
    out_ref[...] = cot + product(row_parts, solved)

    for copies in scatters + lifts + spreads:
        for copy in copies:
            copy.wait_send()


def on_device(n_outer, n_inner, leaf_q, q_cot, leaf_tri, node_blocks, node_tri, root_cot):
    fanins = fan_list(n_outer, n_inner)
    levels = len(fanins)
    order = leaf_tri.shape[1]
    groups = scatter_groups(fanins, order)
    merged = len(groups)
    lifted = levels - merged
    widest = max(fanins[merged:]) - 1
    near = groups[-1] - 1
    dma = pltpu.SemaphoreType.DMA
    args = (leaf_q, q_cot, leaf_tri, node_blocks, node_tri, root_cot)
    return pl.pallas_call(
        functools.partial(kernel, n_outer, n_inner),
        out_shape=jax.ShapeDtypeStruct(leaf_q.shape, F32),
        in_specs=[pl.BlockSpec(memory_space=pltpu.HBM)] * len(args),
        out_specs=pl.BlockSpec(memory_space=pltpu.VMEM),
        scratch_shapes=[pltpu.VMEM(arg.shape, arg.dtype) for arg in args]
        + [
            pltpu.VMEM((merged, order, order), F32),
            pltpu.VMEM((merged, near, order // groups[0], order), F32),
            pltpu.VMEM((lifted, order // groups[-1], order), F32),
            pltpu.VMEM((lifted, widest, order // groups[-1], order), F32),
            pltpu.VMEM((levels, order, order), F32),
            dma((len(args),)),
            dma((merged, near)),
            dma((merged, near)),
            dma((lifted, widest)),
            dma((lifted, widest)),
            dma((levels, near)),
            dma((levels, near)),
        ],
        compiler_params=pltpu.CompilerParams(
            collective_id=0, has_side_effects=True, vmem_limit_bytes=32 * 2**20
        ),
    )(*[pltpu.with_memory_space_constraint(arg, pltpu.HBM) for arg in args])


def solution(mesh):
    return jax.shard_map(
        functools.partial(on_device, mesh.shape["outer"], mesh.shape["inner"]),
        mesh=mesh,
        in_specs=(
            P(("outer", "inner"), None),
            P(("outer", "inner"), None),
            P(("outer", "inner"), None),
            P(None, ("outer", "inner"), None),
            P(None, ("outer", "inner"), None),
            P(),
        ),
        out_specs=P(("outer", "inner"), None),
        check_vma=False,
    )
```

```python
import functools

import jax
import jax.numpy as jnp
from jax import lax
from jax.experimental import pallas as pl
from jax.experimental.pallas import tpu as pltpu
from jax.sharding import PartitionSpec as P

BLOCK = 32
MESH = pl.DeviceIdType.MESH
F32 = jnp.float32
BF16 = jnp.bfloat16


def split(value):
    high = value.astype(BF16)
    return high, (value - high.astype(F32)).astype(BF16)


def product(left, right, turn_right=False):
    left_high, left_low = left
    right_high, right_low = right
    width = right_high.shape[0 if turn_right else 1]
    along, across = (1, 0) if turn_right else (0, 1)
    wide = right_high
    if right_low is not None:
        wide = jnp.concatenate([right_high, right_low], axis=across)
    if left_low is not None:
        wide = jnp.concatenate([wide, wide], axis=along)
        left_high = jnp.concatenate([left_high, left_low], axis=1)
    total = lax.dot_general(
        left_high, wide, (((1,), (along,)), ((), ())), preferred_element_type=F32
    )
    if right_low is not None:
        total = total[:, :width] + total[:, width:]
    return total


def places(order):
    rows = lax.broadcasted_iota(jnp.int32, (order, order), 0)
    columns = lax.broadcasted_iota(jnp.int32, (order, order), 1)
    return rows, columns


def mirror_lower(matrix, rows, columns):
    below = jnp.where(rows > columns, matrix, 0.0)
    return jnp.where(rows >= columns, matrix, 0.0) + below.T


def unpack(parts, inside):
    copies = inside.shape[0] // parts[0].shape[0]
    return tuple(jnp.concatenate([part] * copies, axis=0) * inside for part in parts)


def fold(matrix, span):
    total = matrix[:span]
    for start in range(span, matrix.shape[0], span):
        total = total + matrix[start : start + span]
    return total


def block_inverses(triangles, rows, columns):
    same = rows // BLOCK == columns // BLOCK
    inside = jnp.where(same, 1.0, 0.0).astype(BF16)
    on_diagonal = rows == columns
    eye = fold(jnp.where(on_diagonal, 1.0, 0.0), BLOCK)
    stacks, scales = [], []
    for triangle in triangles:
        diagonal = jnp.where(on_diagonal, triangle, 0.0)
        down = jnp.sum(diagonal, axis=1, keepdims=True)
        scales.append(jnp.sum(diagonal, axis=0, keepdims=True))
        nilpotent = fold(jnp.where(same & (rows < columns), -triangle, 0.0) / down, BLOCK)
        stacks.append((nilpotent, eye + nilpotent))
    power = 2
    while power < BLOCK:
        following = []
        for nilpotent, total in stacks:
            parts = split(nilpotent)
            if power == 2:
                following.append((product(parts, unpack(parts, inside)), total))
                continue
            stacked = split(jnp.concatenate([nilpotent, total], axis=0))
            both = product(stacked, unpack(parts, inside))
            following.append((both[:BLOCK], total + both[BLOCK:]))
        stacks = following
        power = power * 2
    return [
        (total + product(split(total), unpack(split(nilpotent), inside))) / scale
        for (nilpotent, total), scale in zip(stacks, scales)
    ]


def join_inverses(inverses, triangle_parts, rows, columns):
    order = rows.shape[0]
    span = BLOCK
    while span < order:
        row_block, column_block = rows // span, columns // span
        corner = (rows // (2 * span) == columns // (2 * span)) & (row_block < column_block)
        corner = jnp.where(corner, 1.0, 0.0).astype(BF16)
        inside = jnp.where(row_block == column_block, 1.0, 0.0).astype(BF16)
        even = lax.rem(column_block[:span], 2) == 0
        joined = []
        for inverse, (high, low) in zip(inverses, triangle_parts):
            edge = (high * corner, None if low is None else low * corner)
            upper = split(jnp.where(even, inverse, 0.0))
            link = product(split(product(upper, edge)), unpack(split(inverse), inside))
            top = jnp.where(even, inverse, -link)
            joined.append(jnp.concatenate([top, jnp.where(even, 0.0, inverse)], axis=0))
        inverses = joined
        span = span * 2
    return inverses


def fan_list(n_outer, n_inner):
    fanins = []
    remain = n_inner
    while remain > 1:
        fanins.append(min(remain, 4))
        remain = remain // fanins[-1]
    fanins.append(n_outer)
    return fanins


def scatter_groups(fanins, order):
    groups = [fanins[0]]
    if len(fanins) > 2 and order % (8 * fanins[0] * fanins[1]) == 0:
        groups.append(fanins[0] * fanins[1])
    return groups


def add_all(terms):
    while len(terms) > 1:
        pairs = [left + right for left, right in zip(terms[::2], terms[1::2])]
        terms = pairs + terms[len(terms) & ~1 :]
    return terms[0]


def kernel(
    n_outer, n_inner,
    q_hbm, g_hbm, leaf_hbm, blocks_hbm, tri_hbm, root_hbm, out_ref,
    q_ref, g_ref, leaf_ref, blocks_ref, tri_ref, root_ref,
    part_ref, scatter_ref, lift_ref, land_ref, full_ref,
    in_sem, scatter_send, scatter_recv, lift_send, lift_recv, full_send, full_recv,
):
    fanins = fan_list(n_outer, n_inner)
    levels = len(fanins)
    groups = scatter_groups(fanins, leaf_ref.shape[1])
    merged = len(groups)
    outer, inner = lax.axis_index("outer"), lax.axis_index("inner")
    order = leaf_ref.shape[1]

    def near(size, step):
        mine = lax.rem(inner, size)
        other = lax.rem(mine + step, size)
        return other, (outer, inner + other - mine)

    def above(level, step):
        if level == levels - 1:
            return (lax.rem(outer + step, n_outer), inner)
        stride = 1
        for factor in fanins[:level]:
            stride = stride * factor
        mine = lax.rem(inner // stride, fanins[level])
        other = lax.rem(mine + step, fanins[level])
        return (outer, inner + (other - mine) * stride)

    def own_rows(size):
        rows_each = order // size
        return pl.ds(pl.multiple_of(lax.rem(inner, size) * rows_each, rows_each), rows_each)

    loads = [
        pltpu.make_async_copy(source, target, in_sem.at[k])
        for k, (source, target) in enumerate(
            [
                (g_hbm, g_ref), (q_hbm, q_ref), (blocks_hbm, blocks_ref),
                (leaf_hbm, leaf_ref), (tri_hbm, tri_ref), (root_hbm, root_ref),
            ]
        )
    ]
    for load in loads:
        load.start()
    barrier = pltpu.get_barrier_semaphore()
    greeted = [near(groups[-1], step)[1] for step in range(1, groups[-1])]
    for level in range(merged, levels):
        greeted += [above(level, step) for step in range(1, fanins[level])]
    for device in greeted:
        pl.semaphore_signal(barrier, inc=1, device_id=device, device_id_type=MESH)

    def send(source, target, send_sem, recv_sem, device):
        copy = pltpu.make_async_remote_copy(
            src_ref=source, dst_ref=target, send_sem=send_sem, recv_sem=recv_sem,
            device_id=device, device_id_type=MESH,
        )
        copy.start()
        return copy

    def scatter(level):
        size = groups[level]
        rows_each = order // size
        copies = []
        for step in range(1, size):
            other, device = near(size, step)
            copies.append(
                send(
                    part_ref.at[level, pl.ds(pl.multiple_of(other * rows_each, rows_each), rows_each)],
                    scatter_ref.at[level, step - 1, pl.ds(0, rows_each)],
                    scatter_send.at[level, step - 1], scatter_recv.at[level, step - 1], device,
                )
            )
        return copies

    def gathered(level, copies):
        size = groups[level]
        for copy in copies:
            copy.wait_recv()
        terms = [part_ref[level, own_rows(size), :]]
        terms += [scatter_ref[level, step, : order // size] for step in range(size - 1)]
        return add_all(terms)

    def lift(level, value):
        slot = level - merged
        lift_ref[slot] = value
        return [
            send(
                lift_ref.at[slot], land_ref.at[slot, step - 1],
                lift_send.at[slot, step - 1], lift_recv.at[slot, step - 1], above(level, step),
            )
            for step in range(1, fanins[level])
        ]

    def spread(level, value):
        size = groups[min(level, merged - 1)]
        own = own_rows(size)
        full_ref[level, own, :] = value
        return [
            send(
                full_ref.at[level, own], full_ref.at[level, own],
                full_send.at[level, step - 1], full_recv.at[level, step - 1], near(size, step)[1],
            )
            for step in range(1, size)
        ]

    rows, columns = places(order)
    for load in loads[:3]:
        load.wait()
    blocks = [blocks_ref[level] for level in range(levels)]
    leaf_sum = product(split(g_ref[...].T), split(q_ref[...]))
    leaf_parts = split(leaf_sum)
    climbs = [(blocks[0], None)]
    for level in range(1, merged):
        climbs.append(split(product(climbs[-1], (blocks[level], None))))
    part_ref[merged - 1] = product(leaf_parts, climbs[merged - 1])
    pl.semaphore_wait(barrier, len(greeted))
    scatters = [None] * merged
    for level in reversed(range(merged)):
        if level < merged - 1:
            part_ref[level] = product(leaf_parts, climbs[level])
        scatters[level] = scatter(level)

    path = [None] * levels
    path[levels - 1] = (blocks[levels - 1], None)
    for level in reversed(range(levels - 1)):
        path[level] = split(product((blocks[level], None), path[level + 1]))
    for load in loads[3:]:
        load.wait()
    triangles = [leaf_ref[...]] + [tri_ref[level].astype(F32) for level in range(levels)]
    triangle_parts = [split(triangles[0])] + [(tri_ref[level], None) for level in range(levels)]
    inverses = block_inverses(triangles, rows, columns)

    lifts, spreads = [], [None] * levels
    total = gathered(merged - 1, scatters[merged - 1])
    for level in range(merged, levels):
        value = product(split(total), (blocks[level], None))
        lifts.append(lift(level, value))
        spreads[level - 1] = spread(level - 1, total)
        if level == merged:
            inverse_parts = [
                split(inverse)
                for inverse in join_inverses(inverses, triangle_parts, rows, columns)
            ]
        for copy in lifts[-1]:
            copy.wait_recv()
        terms = [lift_ref[level - merged]]
        terms += [land_ref[level - merged, step] for step in range(fanins[level] - 1)]
        total = add_all(terms)
    spreads[levels - 1] = spread(levels - 1, total)

    for level in reversed(range(merged - 1)):
        spreads[level] = spread(level, gathered(level, scatters[level]))

    top = product(triangle_parts[levels], split(root_ref[...]), True)
    cot = product(split(g_ref[...]), split(product(inverse_parts[0], path[0])), True)
    row_parts = split(q_ref[...])
    ratio, weight = [], []
    for level in range(levels):
        carried = product(triangle_parts[level], inverse_parts[level + 1])
        ratio.append(split(carried))
        through = path[level][0].astype(F32)
        if path[level][1] is not None:
            through = through + path[level][1].astype(F32)
        if level < levels - 1:
            carried = product(ratio[level], path[level + 1])
        weight.append(split(carried - through))

    def known_term(level):
        for copy in spreads[level - 1]:
            copy.wait_recv()
        return product(weight[level], split(full_ref[level - 1]))

    known = [product(weight[0], leaf_parts)] + [None] * (levels - 1)
    for level in range(merged, levels):
        known[level] = known_term(level)

    for copy in spreads[levels - 1]:
        copy.wait_recv()
    middle = top - full_ref[levels - 1]
    for level in reversed(range(levels)):
        if known[level] is None:
            known[level] = known_term(level)
        mirrored = split(mirror_lower(middle, rows, columns))
        turned = product(mirrored, (blocks[level], None), True)
        middle = known[level] + product(ratio[level], split(turned))
    mirrored = split(mirror_lower(middle, rows, columns))
    solved = split(product(mirrored, inverse_parts[0], True))
    out_ref[...] = cot + product(row_parts, solved)

    for copies in scatters + lifts + spreads:
        for copy in copies:
            copy.wait_send()


def on_device(n_outer, n_inner, leaf_q, q_cot, leaf_tri, node_blocks, node_tri, root_cot):
    fanins = fan_list(n_outer, n_inner)
    levels = len(fanins)
    order = leaf_tri.shape[1]
    groups = scatter_groups(fanins, order)
    merged = len(groups)
    lifted = levels - merged
    widest = max(fanins[merged:]) - 1
    near = groups[-1] - 1
    dma = pltpu.SemaphoreType.DMA
    args = (leaf_q, q_cot, leaf_tri, node_blocks, node_tri, root_cot)
    return pl.pallas_call(
        functools.partial(kernel, n_outer, n_inner),
        out_shape=jax.ShapeDtypeStruct(leaf_q.shape, F32),
        in_specs=[pl.BlockSpec(memory_space=pltpu.HBM)] * len(args),
        out_specs=pl.BlockSpec(memory_space=pltpu.VMEM),
        scratch_shapes=[pltpu.VMEM(arg.shape, arg.dtype) for arg in args]
        + [
            pltpu.VMEM((merged, order, order), F32),
            pltpu.VMEM((merged, near, order // groups[0], order), F32),
            pltpu.VMEM((lifted, order // groups[-1], order), F32),
            pltpu.VMEM((lifted, widest, order // groups[-1], order), F32),
            pltpu.VMEM((levels, order, order), F32),
            dma((len(args),)),
            dma((merged, near)),
            dma((merged, near)),
            dma((lifted, widest)),
            dma((lifted, widest)),
            dma((levels, near)),
            dma((levels, near)),
        ],
        compiler_params=pltpu.CompilerParams(
            collective_id=0, has_side_effects=True, vmem_limit_bytes=32 * 2**20
        ),
    )(*[pltpu.with_memory_space_constraint(arg, pltpu.HBM) for arg in args])


def solution(mesh):
    return jax.shard_map(
        functools.partial(on_device, mesh.shape["outer"], mesh.shape["inner"]),
        mesh=mesh,
        in_specs=(
            P(("outer", "inner"), None),
            P(("outer", "inner"), None),
            P(("outer", "inner"), None),
            P(None, ("outer", "inner"), None),
            P(None, ("outer", "inner"), None),
            P(),
        ),
        out_specs=P(("outer", "inner"), None),
        check_vma=False,
    )
```

```python
import functools

import jax
import jax.numpy as jnp
from jax import lax
from jax.experimental import pallas as pl
from jax.experimental.pallas import tpu as pltpu
from jax.sharding import PartitionSpec as P

BLOCK = 32
MESH = pl.DeviceIdType.MESH
F32 = jnp.float32
BF16 = jnp.bfloat16


def split(value):
    high = value.astype(BF16)
    return high, (value - high.astype(F32)).astype(BF16)


def keep(ref, parts):
    ref[0], ref[1] = parts


def kept(ref):
    return ref[0], ref[1]


def product(left, right, turn_right=False):
    left_high, left_low = left
    right_high, right_low = right
    width = right_high.shape[0 if turn_right else 1]
    along, across = (1, 0) if turn_right else (0, 1)
    wide = right_high
    if right_low is not None:
        wide = jnp.concatenate([right_high, right_low], axis=across)
    if left_low is not None:
        wide = jnp.concatenate([wide, wide], axis=along)
        left_high = jnp.concatenate([left_high, left_low], axis=1)
    total = lax.dot_general(
        left_high, wide, (((1,), (along,)), ((), ())), preferred_element_type=F32
    )
    if right_low is not None:
        total = total[:, :width] + total[:, width:]
    return total


def places(order):
    rows = lax.broadcasted_iota(jnp.int32, (order, order), 0)
    columns = lax.broadcasted_iota(jnp.int32, (order, order), 1)
    return rows, columns


def mirror_lower(matrix, rows, columns):
    below = jnp.where(rows > columns, matrix, 0.0)
    return jnp.where(rows >= columns, matrix, 0.0) + below.T


def unpack(parts, inside):
    copies = inside.shape[0] // parts[0].shape[0]
    return tuple(jnp.concatenate([part] * copies, axis=0) * inside for part in parts)


def fold(matrix, span):
    total = matrix[:span]
    for start in range(span, matrix.shape[0], span):
        total = total + matrix[start : start + span]
    return total


def block_inverses(triangles, rows, columns):
    same = rows // BLOCK == columns // BLOCK
    inside = jnp.where(same, 1.0, 0.0).astype(BF16)
    on_diagonal = rows == columns
    eye = fold(jnp.where(on_diagonal, 1.0, 0.0), BLOCK)
    stacks, scales = [], []
    for triangle in triangles:
        diagonal = jnp.where(on_diagonal, triangle, 0.0)
        down = jnp.sum(diagonal, axis=1, keepdims=True)
        scales.append(jnp.sum(diagonal, axis=0, keepdims=True))
        nilpotent = fold(jnp.where(same & (rows < columns), -triangle, 0.0) / down, BLOCK)
        stacks.append((nilpotent, eye + nilpotent))
    power = 2
    while power < BLOCK:
        following = []
        for nilpotent, total in stacks:
            parts = split(nilpotent)
            if power == 2:
                following.append((product(parts, unpack(parts, inside)), total))
                continue
            stacked = split(jnp.concatenate([nilpotent, total], axis=0))
            both = product(stacked, unpack(parts, inside))
            following.append((both[:BLOCK], total + both[BLOCK:]))
        stacks = following
        power = power * 2
    return [
        (total + product(split(total), unpack(split(nilpotent), inside))) / scale
        for (nilpotent, total), scale in zip(stacks, scales)
    ]


def join_inverses(inverses, triangle_parts, rows, columns):
    order = rows.shape[0]
    span = BLOCK
    while span < order:
        row_block, column_block = rows // span, columns // span
        corner = (rows // (2 * span) == columns // (2 * span)) & (row_block < column_block)
        corner = jnp.where(corner, 1.0, 0.0).astype(BF16)
        inside = jnp.where(row_block == column_block, 1.0, 0.0).astype(BF16)
        even = lax.rem(column_block[:span], 2) == 0
        joined = []
        for inverse, (high, low) in zip(inverses, triangle_parts):
            edge = (high * corner, None if low is None else low * corner)
            upper = split(jnp.where(even, inverse, 0.0))
            link = product(split(product(upper, edge)), unpack(split(inverse), inside))
            top = jnp.where(even, inverse, -link)
            joined.append(jnp.concatenate([top, jnp.where(even, 0.0, inverse)], axis=0))
        inverses = joined
        span = span * 2
    return inverses


def fan_list(n_outer, n_inner):
    fanins = []
    remain = n_inner
    while remain > 1:
        fanins.append(min(remain, 4))
        remain = remain // fanins[-1]
    fanins.append(n_outer)
    return fanins


def scatter_groups(fanins, order):
    groups = [fanins[0]]
    if len(fanins) > 2 and order % (8 * fanins[0] * fanins[1]) == 0:
        groups.append(fanins[0] * fanins[1])
    return groups


def add_all(terms):
    while len(terms) > 1:
        pairs = [left + right for left, right in zip(terms[::2], terms[1::2])]
        terms = pairs + terms[len(terms) & ~1 :]
    return terms[0]


def kernel(
    n_outer, n_inner,
    q_hbm, g_hbm, leaf_hbm, blocks_hbm, tri_hbm, root_hbm, out_ref,
    q_ref, g_ref, leaf_ref, blocks_ref, tri_ref, root_ref,
    part_ref, scatter_ref, lift_ref, land_ref, full_ref,
    diag_ref, inverse_ref, ratio_ref, weight_ref, sums_ref, below_ref, cot_ref, top_ref,
    in_sem, scatter_send, scatter_recv, lift_send, lift_recv, full_send, full_recv,
):
    fanins = fan_list(n_outer, n_inner)
    levels = len(fanins)
    groups = scatter_groups(fanins, leaf_ref.shape[1])
    merged = len(groups)
    outer, inner = lax.axis_index("outer"), lax.axis_index("inner")
    order = leaf_ref.shape[1]

    def near(size, step):
        mine = lax.rem(inner, size)
        other = lax.rem(mine + step, size)
        return other, (outer, inner + other - mine)

    def above(level, step):
        if level == levels - 1:
            return (lax.rem(outer + step, n_outer), inner)
        stride = 1
        for factor in fanins[:level]:
            stride = stride * factor
        mine = lax.rem(inner // stride, fanins[level])
        other = lax.rem(mine + step, fanins[level])
        return (outer, inner + (other - mine) * stride)

    def own_rows(size):
        rows_each = order // size
        return pl.ds(pl.multiple_of(lax.rem(inner, size) * rows_each, rows_each), rows_each)

    loads = [
        pltpu.make_async_copy(source, target, in_sem.at[k])
        for k, (source, target) in enumerate(
            [
                (g_hbm, g_ref), (q_hbm, q_ref), (blocks_hbm, blocks_ref),
                (leaf_hbm, leaf_ref), (tri_hbm, tri_ref), (root_hbm, root_ref),
            ]
        )
    ]
    for load in loads:
        load.start()
    barrier = pltpu.get_barrier_semaphore()
    greeted = [near(groups[-1], step)[1] for step in range(1, groups[-1])]
    for level in range(merged, levels):
        greeted += [above(level, step) for step in range(1, fanins[level])]
    for device in greeted:
        pl.semaphore_signal(barrier, inc=1, device_id=device, device_id_type=MESH)

    def send(source, target, send_sem, recv_sem, device):
        copy = pltpu.make_async_remote_copy(
            src_ref=source, dst_ref=target, send_sem=send_sem, recv_sem=recv_sem,
            device_id=device, device_id_type=MESH,
        )
        copy.start()
        return copy

    def scatter(level):
        size = groups[level]
        rows_each = order // size
        copies = []
        for step in range(1, size):
            other, device = near(size, step)
            copies.append(
                send(
                    part_ref.at[level, pl.ds(pl.multiple_of(other * rows_each, rows_each), rows_each)],
                    scatter_ref.at[level, step - 1, pl.ds(0, rows_each)],
                    scatter_send.at[level, step - 1], scatter_recv.at[level, step - 1], device,
                )
            )
        return copies

    def gathered(level, copies):
        size = groups[level]
        for copy in copies:
            copy.wait_recv()
        terms = [part_ref[level, own_rows(size), :]]
        terms += [scatter_ref[level, step, : order // size] for step in range(size - 1)]
        return add_all(terms)

    def lift(level, value):
        slot = level - merged
        lift_ref[slot] = value
        return [
            send(
                lift_ref.at[slot], land_ref.at[slot, step - 1],
                lift_send.at[slot, step - 1], lift_recv.at[slot, step - 1], above(level, step),
            )
            for step in range(1, fanins[level])
        ]

    def spread(level, value):
        size = groups[min(level, merged - 1)]
        own = own_rows(size)
        full_ref[level, own, :] = value
        return [
            send(
                full_ref.at[level, own], full_ref.at[level, own],
                full_send.at[level, step - 1], full_recv.at[level, step - 1], near(size, step)[1],
            )
            for step in range(1, size)
        ]

    rows, columns = places(order)
    for load in loads[:3]:
        load.wait()
    blocks = [blocks_ref[level] for level in range(levels)]
    leaf_sum = product(split(g_ref[...].T), split(q_ref[...]))
    leaf_parts = split(leaf_sum)
    keep(sums_ref, leaf_parts)
    climbs = [(blocks[0], None)]
    for level in range(1, merged):
        climbs.append(split(product(climbs[-1], (blocks[level], None))))
    part_ref[merged - 1] = product(leaf_parts, climbs[merged - 1])
    for load in loads[3:]:
        load.wait()

    def invert_blocks():
        triangles = [leaf_ref[...]] + [tri_ref[level].astype(F32) for level in range(levels)]
        for k, inverse in enumerate(block_inverses(triangles, rows, columns)):
            diag_ref[k] = inverse

    def triangle_parts():
        return [split(leaf_ref[...])] + [(tri_ref[level], None) for level in range(levels)]

    def invert():
        inverses = [diag_ref[k] for k in range(levels + 1)]
        for k, inverse in enumerate(join_inverses(inverses, triangle_parts(), rows, columns)):
            keep(inverse_ref.at[k], split(inverse))

    def prepare():
        parts = triangle_parts()
        path = [None] * levels
        path[levels - 1] = (blocks_ref[levels - 1], None)
        for level in reversed(range(levels - 1)):
            path[level] = split(product((blocks_ref[level], None), path[level + 1]))
        for level in range(levels):
            carried = product(parts[level], kept(inverse_ref.at[level + 1]))
            ratio = split(carried)
            keep(ratio_ref.at[level], ratio)
            through = path[level][0].astype(F32)
            if path[level][1] is not None:
                through = through + path[level][1].astype(F32)
            if level < levels - 1:
                carried = product(ratio, path[level + 1])
            weight = split(carried - through)
            if level == 0:
                below_ref[...] = product(weight, kept(sums_ref))
            else:
                keep(weight_ref.at[level], weight)
        top_ref[...] = product(parts[levels], split(root_ref[...]), True)
        cot_path = split(product(kept(inverse_ref.at[0]), path[0]))
        cot_ref[...] = product(split(g_ref[...]), cot_path, True)

    ahead = inner < n_inner // 2
    pl.when(ahead)(invert_blocks)
    pl.semaphore_wait(barrier, len(greeted))
    scatters = [None] * merged
    for level in reversed(range(merged)):
        if level < merged - 1:
            part_ref[level] = product(leaf_parts, climbs[level])
        scatters[level] = scatter(level)
    pl.when(ahead)(invert)

    lifts, spreads = [], [None] * levels
    total = gathered(merged - 1, scatters[merged - 1])
    for level in range(merged, levels):
        value = product(split(total), (blocks[level], None))
        lifts.append(lift(level, value))
        spreads[level - 1] = spread(level - 1, total)
        if level == merged:
            for below in reversed(range(merged - 1)):
                spreads[below] = spread(below, gathered(below, scatters[below]))
            pl.when(ahead)(prepare)
        for copy in lifts[-1]:
            copy.wait_recv()
        terms = [lift_ref[level - merged]]
        terms += [land_ref[level - merged, step] for step in range(fanins[level] - 1)]
        total = add_all(terms)
    spreads[levels - 1] = spread(levels - 1, total)

    @pl.when(jnp.logical_not(ahead))
    def work_late():
        invert_blocks()
        invert()
        prepare()

    for level in range(levels - 1):
        for copy in spreads[level]:
            copy.wait_recv()
    known = [below_ref[...]]
    for level in range(1, levels):
        known.append(product(kept(weight_ref.at[level]), split(full_ref[level - 1])))
    row_parts = split(q_ref[...])
    ratio = [kept(ratio_ref.at[level]) for level in range(levels)]

    for copy in spreads[levels - 1]:
        copy.wait_recv()
    middle = top_ref[...] - full_ref[levels - 1]
    for level in reversed(range(levels)):
        mirrored = split(mirror_lower(middle, rows, columns))
        turned = product(mirrored, (blocks[level], None), True)
        middle = known[level] + product(ratio[level], split(turned))
    mirrored = split(mirror_lower(middle, rows, columns))
    solved = split(product(mirrored, kept(inverse_ref.at[0]), True))
    out_ref[...] = cot_ref[...] + product(row_parts, solved)

    for copies in scatters + lifts + spreads:
        for copy in copies:
            copy.wait_send()


def on_device(n_outer, n_inner, leaf_q, q_cot, leaf_tri, node_blocks, node_tri, root_cot):
    fanins = fan_list(n_outer, n_inner)
    levels = len(fanins)
    order = leaf_tri.shape[1]
    groups = scatter_groups(fanins, order)
    merged = len(groups)
    lifted = levels - merged
    widest = max(fanins[merged:]) - 1
    near = groups[-1] - 1
    dma = pltpu.SemaphoreType.DMA
    args = (leaf_q, q_cot, leaf_tri, node_blocks, node_tri, root_cot)
    return pl.pallas_call(
        functools.partial(kernel, n_outer, n_inner),
        out_shape=jax.ShapeDtypeStruct(leaf_q.shape, F32),
        in_specs=[pl.BlockSpec(memory_space=pltpu.HBM)] * len(args),
        out_specs=pl.BlockSpec(memory_space=pltpu.VMEM),
        scratch_shapes=[pltpu.VMEM(arg.shape, arg.dtype) for arg in args]
        + [
            pltpu.VMEM((merged, order, order), F32),
            pltpu.VMEM((merged, near, order // groups[0], order), F32),
            pltpu.VMEM((lifted, order // groups[-1], order), F32),
            pltpu.VMEM((lifted, widest, order // groups[-1], order), F32),
            pltpu.VMEM((levels, order, order), F32),
            pltpu.VMEM((levels + 1, BLOCK, order), F32),
            pltpu.VMEM((levels + 1, 2, order, order), BF16),
            pltpu.VMEM((levels, 2, order, order), BF16),
            pltpu.VMEM((levels, 2, order, order), BF16),
            pltpu.VMEM((2, order, order), BF16),
            pltpu.VMEM((order, order), F32),
            pltpu.VMEM(leaf_q.shape, F32),
            pltpu.VMEM((order, order), F32),
            dma((len(args),)),
            dma((merged, near)),
            dma((merged, near)),
            dma((lifted, widest)),
            dma((lifted, widest)),
            dma((levels, near)),
            dma((levels, near)),
        ],
        compiler_params=pltpu.CompilerParams(
            collective_id=0, has_side_effects=True, vmem_limit_bytes=32 * 2**20
        ),
    )(*[pltpu.with_memory_space_constraint(arg, pltpu.HBM) for arg in args])


def solution(mesh):
    return jax.shard_map(
        functools.partial(on_device, mesh.shape["outer"], mesh.shape["inner"]),
        mesh=mesh,
        in_specs=(
            P(("outer", "inner"), None),
            P(("outer", "inner"), None),
            P(("outer", "inner"), None),
            P(None, ("outer", "inner"), None),
            P(None, ("outer", "inner"), None),
            P(),
        ),
        out_specs=P(("outer", "inner"), None),
        check_vma=False,
    )
```

```python
import functools

import jax
import jax.numpy as jnp
from jax import lax
from jax.experimental import pallas as pl
from jax.experimental.pallas import tpu as pltpu
from jax.sharding import PartitionSpec as P

BLOCK = 32
MESH = pl.DeviceIdType.MESH
F32 = jnp.float32
BF16 = jnp.bfloat16


def split(value):
    high = value.astype(BF16)
    return high, (value - high.astype(F32)).astype(BF16)


def product(left, right, turn_right=False):
    left_high, left_low = left
    right_high, right_low = right
    width = right_high.shape[0 if turn_right else 1]
    along, across = (1, 0) if turn_right else (0, 1)
    wide = right_high
    if right_low is not None:
        wide = jnp.concatenate([right_high, right_low], axis=across)
    if left_low is not None:
        wide = jnp.concatenate([wide, wide], axis=along)
        left_high = jnp.concatenate([left_high, left_low], axis=1)
    total = lax.dot_general(
        left_high, wide, (((1,), (along,)), ((), ())), preferred_element_type=F32
    )
    if right_low is not None:
        total = total[:, :width] + total[:, width:]
    return total


def places(order):
    rows = lax.broadcasted_iota(jnp.int32, (order, order), 0)
    columns = lax.broadcasted_iota(jnp.int32, (order, order), 1)
    return rows, columns


def mirror_lower(matrix, rows, columns):
    below = jnp.where(rows > columns, matrix, 0.0)
    return jnp.where(rows >= columns, matrix, 0.0) + below.T


def unpack(parts, inside):
    copies = inside.shape[0] // parts[0].shape[0]
    return tuple(jnp.concatenate([part] * copies, axis=0) * inside for part in parts)


def fold(matrix, span):
    total = matrix[:span]
    for start in range(span, matrix.shape[0], span):
        total = total + matrix[start : start + span]
    return total


def block_inverses(triangles, rows, columns):
    same = rows // BLOCK == columns // BLOCK
    inside = jnp.where(same, 1.0, 0.0).astype(BF16)
    on_diagonal = rows == columns
    eye = fold(jnp.where(on_diagonal, 1.0, 0.0), BLOCK)
    stacks, scales = [], []
    for triangle in triangles:
        diagonal = jnp.where(on_diagonal, triangle, 0.0)
        down = jnp.sum(diagonal, axis=1, keepdims=True)
        scales.append(jnp.sum(diagonal, axis=0, keepdims=True))
        nilpotent = fold(jnp.where(same & (rows < columns), -triangle, 0.0) / down, BLOCK)
        stacks.append((nilpotent, eye + nilpotent))
    power = 2
    while power < BLOCK:
        following = []
        for nilpotent, total in stacks:
            parts = split(nilpotent)
            if power == 2:
                following.append((product(parts, unpack(parts, inside)), total))
                continue
            stacked = split(jnp.concatenate([nilpotent, total], axis=0))
            both = product(stacked, unpack(parts, inside))
            following.append((both[:BLOCK], total + both[BLOCK:]))
        stacks = following
        power = power * 2
    return [
        (total + product(split(total), unpack(split(nilpotent), inside))) / scale
        for (nilpotent, total), scale in zip(stacks, scales)
    ]


def join_inverses(inverses, triangle_parts, rows, columns):
    order = rows.shape[0]
    span = BLOCK
    while span < order:
        row_block, column_block = rows // span, columns // span
        corner = (rows // (2 * span) == columns // (2 * span)) & (row_block < column_block)
        corner = jnp.where(corner, 1.0, 0.0).astype(BF16)
        inside = jnp.where(row_block == column_block, 1.0, 0.0).astype(BF16)
        even = lax.rem(column_block[:span], 2) == 0
        joined = []
        for inverse, (high, low) in zip(inverses, triangle_parts):
            edge = (high * corner, None if low is None else low * corner)
            upper = split(jnp.where(even, inverse, 0.0))
            link = product(split(product(upper, edge)), unpack(split(inverse), inside))
            top = jnp.where(even, inverse, -link)
            joined.append(jnp.concatenate([top, jnp.where(even, 0.0, inverse)], axis=0))
        inverses = joined
        span = span * 2
    return inverses


def fan_list(n_outer, n_inner):
    fanins = []
    remain = n_inner
    while remain > 1:
        fanins.append(min(remain, 4))
        remain = remain // fanins[-1]
    fanins.append(n_outer)
    return fanins


def add_all(terms):
    while len(terms) > 1:
        pairs = [left + right for left, right in zip(terms[::2], terms[1::2])]
        terms = pairs + terms[len(terms) & ~1 :]
    return terms[0]


def kernel(
    n_outer, n_inner,
    q_hbm, g_hbm, leaf_hbm, blocks_hbm, tri_hbm, root_hbm, out_ref,
    q_ref, g_ref, leaf_ref, blocks_ref, tri_ref, root_ref,
    part_ref, scatter_ref, lift_ref, land_ref, full_ref,
    top_ref, far_ref, reach_ref,
    in_sem, top_send, top_recv, far_send, far_recv, join_send, join_recv,
    scatter_send, scatter_recv, lift_send, lift_recv, full_send, full_recv,
):
    fanins = fan_list(n_outer, n_inner)
    levels = len(fanins)
    groups, merged = [fanins[0]], 1
    outer, inner = lax.axis_index("outer"), lax.axis_index("inner")
    order = leaf_ref.shape[1]

    def near(size, step):
        mine = lax.rem(inner, size)
        other = lax.rem(mine + step, size)
        return other, (outer, inner + other - mine)

    def above(level, step):
        if level == levels - 1:
            return (lax.rem(outer + step, n_outer), inner)
        stride = 1
        for factor in fanins[:level]:
            stride = stride * factor
        mine = lax.rem(inner // stride, fanins[level])
        other = lax.rem(mine + step, fanins[level])
        return (outer, inner + (other - mine) * stride)

    beside = min(2, n_inner)
    team = n_outer * beside
    team_rows = order // team
    others = n_inner // beside

    def team_place(step):
        mine = outer * beside + lax.rem(inner, beside)
        other = lax.rem(mine + step, team)
        return other, (other // beside, inner - lax.rem(inner, beside) + lax.rem(other, beside))

    def far_device(step):
        return (outer, lax.rem(inner + beside * step, n_inner))

    def team_slice(place):
        return pl.ds(pl.multiple_of(place * team_rows, team_rows), team_rows)

    def own_rows(size):
        rows_each = order // size
        return pl.ds(pl.multiple_of(lax.rem(inner, size) * rows_each, rows_each), rows_each)

    loads = [
        pltpu.make_async_copy(source, target, in_sem.at[k])
        for k, (source, target) in enumerate(
            [
                (g_hbm, g_ref), (q_hbm, q_ref), (blocks_hbm, blocks_ref),
                (leaf_hbm, leaf_ref), (tri_hbm, tri_ref), (root_hbm, root_ref),
            ]
        )
    ]
    for load in loads:
        load.start()
    barrier = pltpu.get_barrier_semaphore()
    greeted = [near(groups[-1], step)[1] for step in range(1, groups[-1])]
    for level in range(merged, levels - 1):
        greeted += [above(level, step) for step in range(1, fanins[level])]
    greeted += [team_place(step)[1] for step in range(1, team)]
    greeted += [far_device(step) for step in range(1, others)]
    for device in greeted:
        pl.semaphore_signal(barrier, inc=1, device_id=device, device_id_type=MESH)

    def send(source, target, send_sem, recv_sem, device):
        copy = pltpu.make_async_remote_copy(
            src_ref=source, dst_ref=target, send_sem=send_sem, recv_sem=recv_sem,
            device_id=device, device_id_type=MESH,
        )
        copy.start()
        return copy

    def scatter(level):
        size = groups[level]
        rows_each = order // size
        copies = []
        for step in range(1, size):
            other, device = near(size, step)
            copies.append(
                send(
                    part_ref.at[level, pl.ds(pl.multiple_of(other * rows_each, rows_each), rows_each)],
                    scatter_ref.at[level, step - 1, pl.ds(0, rows_each)],
                    scatter_send.at[level, step - 1], scatter_recv.at[level, step - 1], device,
                )
            )
        return copies

    def gathered(level, copies):
        size = groups[level]
        for copy in copies:
            copy.wait_recv()
        terms = [part_ref[level, own_rows(size), :]]
        terms += [scatter_ref[level, step, : order // size] for step in range(size - 1)]
        return add_all(terms)

    def lift(level, value):
        slot = level - merged
        lift_ref[slot] = value
        return [
            send(
                lift_ref.at[slot], land_ref.at[slot, step - 1],
                lift_send.at[slot, step - 1], lift_recv.at[slot, step - 1], above(level, step),
            )
            for step in range(1, fanins[level])
        ]

    def spread(level, value):
        size = groups[min(level, merged - 1)]
        own = own_rows(size)
        full_ref[level, own, :] = value
        return [
            send(
                full_ref.at[level, own], full_ref.at[level, own],
                full_send.at[level, step - 1], full_recv.at[level, step - 1], near(size, step)[1],
            )
            for step in range(1, size)
        ]

    rows, columns = places(order)
    for load in loads[:3]:
        load.wait()
    blocks = [blocks_ref[level] for level in range(levels)]
    leaf_sum = product(split(g_ref[...].T), split(q_ref[...]))
    leaf_parts = split(leaf_sum)
    path = [None] * levels
    path[levels - 1] = (blocks[levels - 1], None)
    for level in reversed(range(levels - 1)):
        path[level] = split(product((blocks[level], None), path[level + 1]))
    top_ref[...] = product(leaf_parts, path[0])
    pl.semaphore_wait(barrier, len(greeted))
    shares = []
    for step in range(1, team):
        other, device = team_place(step)
        shares.append(
            send(
                top_ref.at[team_slice(other)], reach_ref.at[step - 1],
                top_send.at[step - 1], top_recv.at[step - 1], device,
            )
        )
    part_ref[0] = product(leaf_parts, (blocks[0], None))
    scatters = [scatter(0)]

    for load in loads[3:]:
        load.wait()
    triangles = [leaf_ref[...]] + [tri_ref[level].astype(F32) for level in range(levels)]
    triangle_parts = [split(triangles[0])] + [(tri_ref[level], None) for level in range(levels)]
    inverses = block_inverses(triangles, rows, columns)

    lifts, spreads = [], [None] * (levels - 1)
    mine = team_slice(team_place(0)[0])
    for copy in shares:
        copy.wait_recv()
    far_ref[0] = add_all([top_ref[mine, :]] + [reach_ref[step] for step in range(team - 1)])
    fars = [
        send(
            far_ref.at[0], far_ref.at[step],
            far_send.at[step - 1], far_recv.at[step - 1], far_device(step),
        )
        for step in range(1, others)
    ]
    total = gathered(0, scatters[0])
    if levels > 2:
        lifts.append(lift(1, product(split(total), (blocks[1], None))))
    spreads[0] = spread(0, total)

    inverse_parts = [
        split(inverse) for inverse in join_inverses(inverses, triangle_parts, rows, columns)
    ]
    ratio_sums = [
        product(triangle_parts[level], inverse_parts[level + 1]) for level in range(levels)
    ]
    ratio = [split(value) for value in ratio_sums]

    for copy in fars:
        copy.wait_recv()
    full_ref[levels - 1, mine, :] = add_all([far_ref[step] for step in range(others)])
    joins = [
        send(
            full_ref.at[levels - 1, mine], full_ref.at[levels - 1, mine],
            join_send.at[step - 1], join_recv.at[step - 1], team_place(step)[1],
        )
        for step in range(1, team)
    ]
    for level in range(1, levels - 1):
        for copy in lifts[level - 1]:
            copy.wait_recv()
        terms = [lift_ref[level - 1]]
        terms += [land_ref[level - 1, step] for step in range(fanins[level] - 1)]
        total = add_all(terms)
        if level + 1 < levels - 1:
            lifts.append(lift(level + 1, product(split(total), (blocks[level + 1], None))))
        spreads[level] = spread(level, total)

    top = product(triangle_parts[levels], split(root_ref[...]), True)
    known = []
    for level in range(levels):
        through = path[level][0].astype(F32)
        if path[level][1] is not None:
            through = through + path[level][1].astype(F32)
        carried = ratio_sums[level]
        if level < levels - 1:
            carried = product(ratio[level], path[level + 1])
        if level == 0:
            own_sums = leaf_parts
        else:
            for copy in spreads[level - 1]:
                copy.wait_recv()
            own_sums = split(full_ref[level - 1])
        known.append(product(split(carried - through), own_sums))
    cot = product(split(g_ref[...]), split(product(inverse_parts[0], path[0])), True)
    row_parts = split(q_ref[...])

    for copy in joins:
        copy.wait_recv()
    middle = top - full_ref[levels - 1]
    for level in reversed(range(levels)):
        mirrored = split(mirror_lower(middle, rows, columns))
        turned = product(mirrored, (blocks[level], None), True)
        middle = known[level] + product(ratio[level], split(turned))
    mirrored = split(mirror_lower(middle, rows, columns))
    solved = split(product(mirrored, inverse_parts[0], True))
    out_ref[...] = cot + product(row_parts, solved)

    for copies in scatters + lifts + spreads + [shares, fars, joins]:
        for copy in copies:
            copy.wait_send()


def on_device(n_outer, n_inner, leaf_q, q_cot, leaf_tri, node_blocks, node_tri, root_cot):
    fanins = fan_list(n_outer, n_inner)
    levels = len(fanins)
    order = leaf_tri.shape[1]
    groups, merged = [fanins[0]], 1
    lifted = max(levels - 2, 1)
    widest = max(fanins[1:-1] + [2]) - 1
    team = n_outer * min(2, n_inner)
    others = n_inner // min(2, n_inner)
    near = groups[-1] - 1
    dma = pltpu.SemaphoreType.DMA
    args = (leaf_q, q_cot, leaf_tri, node_blocks, node_tri, root_cot)
    return pl.pallas_call(
        functools.partial(kernel, n_outer, n_inner),
        out_shape=jax.ShapeDtypeStruct(leaf_q.shape, F32),
        in_specs=[pl.BlockSpec(memory_space=pltpu.HBM)] * len(args),
        out_specs=pl.BlockSpec(memory_space=pltpu.VMEM),
        scratch_shapes=[pltpu.VMEM(arg.shape, arg.dtype) for arg in args]
        + [
            pltpu.VMEM((merged, order, order), F32),
            pltpu.VMEM((merged, near, order // groups[0], order), F32),
            pltpu.VMEM((lifted, order // groups[-1], order), F32),
            pltpu.VMEM((lifted, widest, order // groups[-1], order), F32),
            pltpu.VMEM((levels, order, order), F32),
            pltpu.VMEM((order, order), F32),
            pltpu.VMEM((others, order // team, order), F32),
            pltpu.VMEM((team - 1, order // team, order), F32),
            dma((len(args),)),
            dma((team - 1,)),
            dma((team - 1,)),
            dma((max(others - 1, 1),)),
            dma((max(others - 1, 1),)),
            dma((team - 1,)),
            dma((team - 1,)),
            dma((merged, near)),
            dma((merged, near)),
            dma((lifted, widest)),
            dma((lifted, widest)),
            dma((levels, near)),
            dma((levels, near)),
        ],
        compiler_params=pltpu.CompilerParams(
            collective_id=0, has_side_effects=True, vmem_limit_bytes=32 * 2**20
        ),
    )(*[pltpu.with_memory_space_constraint(arg, pltpu.HBM) for arg in args])


def solution(mesh):
    return jax.shard_map(
        functools.partial(on_device, mesh.shape["outer"], mesh.shape["inner"]),
        mesh=mesh,
        in_specs=(
            P(("outer", "inner"), None),
            P(("outer", "inner"), None),
            P(("outer", "inner"), None),
            P(None, ("outer", "inner"), None),
            P(None, ("outer", "inner"), None),
            P(),
        ),
        out_specs=P(("outer", "inner"), None),
        check_vma=False,
    )
```

```python
import functools

import jax
import jax.numpy as jnp
from jax import lax
from jax.experimental import pallas as pl
from jax.experimental.pallas import tpu as pltpu
from jax.sharding import PartitionSpec as P

BLOCK = 32
MESH = pl.DeviceIdType.MESH
F32 = jnp.float32
BF16 = jnp.bfloat16


def split(value):
    high = value.astype(BF16)
    return high, (value - high.astype(F32)).astype(BF16)


def product(left, right, turn_right=False):
    left_high, left_low = left
    right_high, right_low = right
    width = right_high.shape[0 if turn_right else 1]
    along, across = (1, 0) if turn_right else (0, 1)
    wide = right_high
    if right_low is not None:
        wide = jnp.concatenate([right_high, right_low], axis=across)
    if left_low is not None:
        wide = jnp.concatenate([wide, wide], axis=along)
        left_high = jnp.concatenate([left_high, left_low], axis=1)
    total = lax.dot_general(
        left_high, wide, (((1,), (along,)), ((), ())), preferred_element_type=F32
    )
    if right_low is not None:
        total = total[:, :width] + total[:, width:]
    return total


def places(order):
    rows = lax.broadcasted_iota(jnp.int32, (order, order), 0)
    columns = lax.broadcasted_iota(jnp.int32, (order, order), 1)
    return rows, columns


def mirror_lower(matrix, rows, columns):
    below = jnp.where(rows > columns, matrix, 0.0)
    return jnp.where(rows >= columns, matrix, 0.0) + below.T


def unpack(parts, inside):
    copies = inside.shape[0] // parts[0].shape[0]
    return tuple(jnp.concatenate([part] * copies, axis=0) * inside for part in parts)


def fold(matrix, span):
    total = matrix[:span]
    for start in range(span, matrix.shape[0], span):
        total = total + matrix[start : start + span]
    return total


def block_inverses(triangles, rows, columns):
    same = rows // BLOCK == columns // BLOCK
    inside = jnp.where(same, 1.0, 0.0).astype(BF16)
    on_diagonal = rows == columns
    eye = fold(jnp.where(on_diagonal, 1.0, 0.0), BLOCK)
    stacks, scales = [], []
    for triangle in triangles:
        diagonal = jnp.where(on_diagonal, triangle, 0.0)
        down = jnp.sum(diagonal, axis=1, keepdims=True)
        scales.append(jnp.sum(diagonal, axis=0, keepdims=True))
        nilpotent = fold(jnp.where(same & (rows < columns), -triangle, 0.0) / down, BLOCK)
        stacks.append((nilpotent, eye + nilpotent))
    power = 2
    while power < BLOCK:
        following = []
        for nilpotent, total in stacks:
            parts = split(nilpotent)
            if power == 2:
                following.append((product(parts, unpack(parts, inside)), total))
                continue
            stacked = split(jnp.concatenate([nilpotent, total], axis=0))
            both = product(stacked, unpack(parts, inside))
            following.append((both[:BLOCK], total + both[BLOCK:]))
        stacks = following
        power = power * 2
    return [
        (total + product(split(total), unpack(split(nilpotent), inside))) / scale
        for (nilpotent, total), scale in zip(stacks, scales)
    ]


def join_inverses(inverses, triangle_parts, rows, columns):
    order = rows.shape[0]
    span = BLOCK
    while span < order:
        row_block, column_block = rows // span, columns // span
        corner = (rows // (2 * span) == columns // (2 * span)) & (row_block < column_block)
        corner = jnp.where(corner, 1.0, 0.0).astype(BF16)
        inside = jnp.where(row_block == column_block, 1.0, 0.0).astype(BF16)
        even = lax.rem(column_block[:span], 2) == 0
        joined = []
        for inverse, (high, low) in zip(inverses, triangle_parts):
            edge = (high * corner, None if low is None else low * corner)
            upper = split(jnp.where(even, inverse, 0.0))
            link = product(split(product(upper, edge)), unpack(split(inverse), inside))
            top = jnp.where(even, inverse, -link)
            joined.append(jnp.concatenate([top, jnp.where(even, 0.0, inverse)], axis=0))
        inverses = joined
        span = span * 2
    return inverses


def fan_list(n_outer, n_inner):
    fanins = []
    remain = n_inner
    while remain > 1:
        fanins.append(min(remain, 4))
        remain = remain // fanins[-1]
    fanins.append(n_outer)
    return fanins


def add_all(terms):
    while len(terms) > 1:
        pairs = [left + right for left, right in zip(terms[::2], terms[1::2])]
        terms = pairs + terms[len(terms) & ~1 :]
    return terms[0]


def kernel(
    n_outer, n_inner,
    q_hbm, g_hbm, leaf_hbm, blocks_hbm, tri_hbm, root_hbm, out_ref,
    q_ref, g_ref, leaf_ref, blocks_ref, tri_ref, root_ref,
    part_ref, scatter_ref, lift_ref, land_ref, full_ref,
    top_ref, far_ref, reach_ref,
    in_sem, top_send, top_recv, far_send, far_recv, join_send, join_recv,
    scatter_send, scatter_recv, lift_send, lift_recv, full_send, full_recv,
):
    fanins = fan_list(n_outer, n_inner)
    levels = len(fanins)
    groups, merged = [fanins[0]], 1
    outer, inner = lax.axis_index("outer"), lax.axis_index("inner")
    order = leaf_ref.shape[1]

    def near(size, step):
        mine = lax.rem(inner, size)
        other = lax.rem(mine + step, size)
        return other, (outer, inner + other - mine)

    def above(level, step):
        if level == levels - 1:
            return (lax.rem(outer + step, n_outer), inner)
        stride = 1
        for factor in fanins[:level]:
            stride = stride * factor
        mine = lax.rem(inner // stride, fanins[level])
        other = lax.rem(mine + step, fanins[level])
        return (outer, inner + (other - mine) * stride)

    beside = min(2, n_inner)
    team = n_outer * beside
    team_rows = order // team
    others = n_inner // beside

    def team_place(step):
        mine = outer * beside + lax.rem(inner, beside)
        other = lax.rem(mine + step, team)
        return other, (other // beside, inner - lax.rem(inner, beside) + lax.rem(other, beside))

    def far_device(step):
        return (outer, lax.rem(inner + beside * step, n_inner))

    def team_slice(place):
        return pl.ds(pl.multiple_of(place * team_rows, team_rows), team_rows)

    def own_rows(size):
        rows_each = order // size
        return pl.ds(pl.multiple_of(lax.rem(inner, size) * rows_each, rows_each), rows_each)

    loads = [
        pltpu.make_async_copy(source, target, in_sem.at[k])
        for k, (source, target) in enumerate(
            [
                (g_hbm, g_ref), (q_hbm, q_ref), (blocks_hbm, blocks_ref),
                (leaf_hbm, leaf_ref), (tri_hbm, tri_ref), (root_hbm, root_ref),
            ]
        )
    ]
    for load in loads:
        load.start()
    barrier = pltpu.get_barrier_semaphore()
    greeted = [near(groups[-1], step)[1] for step in range(1, groups[-1])]
    for level in range(merged, levels - 1):
        greeted += [above(level, step) for step in range(1, fanins[level])]
    greeted += [team_place(step)[1] for step in range(1, team)]
    greeted += [far_device(step) for step in range(1, others)]
    for device in greeted:
        pl.semaphore_signal(barrier, inc=1, device_id=device, device_id_type=MESH)

    def send(source, target, send_sem, recv_sem, device):
        copy = pltpu.make_async_remote_copy(
            src_ref=source, dst_ref=target, send_sem=send_sem, recv_sem=recv_sem,
            device_id=device, device_id_type=MESH,
        )
        copy.start()
        return copy

    def scatter(level):
        size = groups[level]
        rows_each = order // size
        copies = []
        for step in range(1, size):
            other, device = near(size, step)
            copies.append(
                send(
                    part_ref.at[level, pl.ds(pl.multiple_of(other * rows_each, rows_each), rows_each)],
                    scatter_ref.at[level, step - 1, pl.ds(0, rows_each)],
                    scatter_send.at[level, step - 1], scatter_recv.at[level, step - 1], device,
                )
            )
        return copies

    def gathered(level, copies):
        size = groups[level]
        for copy in copies:
            copy.wait_recv()
        terms = [part_ref[level, own_rows(size), :]]
        terms += [scatter_ref[level, step, : order // size] for step in range(size - 1)]
        return add_all(terms)

    def lift(level, value):
        slot = level - merged
        lift_ref[slot] = value
        return [
            send(
                lift_ref.at[slot], land_ref.at[slot, step - 1],
                lift_send.at[slot, step - 1], lift_recv.at[slot, step - 1], above(level, step),
            )
            for step in range(1, fanins[level])
        ]

    def spread(level, value):
        size = groups[min(level, merged - 1)]
        own = own_rows(size)
        full_ref[level, own, :] = value
        return [
            send(
                full_ref.at[level, own], full_ref.at[level, own],
                full_send.at[level, step - 1], full_recv.at[level, step - 1], near(size, step)[1],
            )
            for step in range(1, size)
        ]

    rows, columns = places(order)
    for load in loads[:3]:
        load.wait()
    blocks = [blocks_ref[level] for level in range(levels)]
    leaf_sum = product(split(g_ref[...].T), split(q_ref[...]))
    leaf_parts = split(leaf_sum)
    path = [None] * levels
    path[levels - 1] = (blocks[levels - 1], None)
    for level in reversed(range(levels - 1)):
        path[level] = split(product((blocks[level], None), path[level + 1]))
    top_ref[...] = product(leaf_parts, path[0])
    pl.semaphore_wait(barrier, len(greeted))
    shares = []
    for step in range(1, team):
        other, device = team_place(step)
        shares.append(
            send(
                top_ref.at[team_slice(other)], reach_ref.at[step - 1],
                top_send.at[step - 1], top_recv.at[step - 1], device,
            )
        )
    part_ref[0] = product(leaf_parts, (blocks[0], None))
    scatters = [scatter(0)]

    for load in loads[3:]:
        load.wait()
    triangles = [leaf_ref[...]] + [tri_ref[level].astype(F32) for level in range(levels)]
    triangle_parts = [split(triangles[0])] + [(tri_ref[level], None) for level in range(levels)]
    inverses = block_inverses(triangles, rows, columns)

    lifts, spreads = [], [None] * (levels - 1)
    mine = team_slice(team_place(0)[0])
    for copy in shares:
        copy.wait_recv()
    far_ref[0] = add_all([top_ref[mine, :]] + [reach_ref[step] for step in range(team - 1)])
    fars = [
        send(
            far_ref.at[0], far_ref.at[step],
            far_send.at[step - 1], far_recv.at[step - 1], far_device(step),
        )
        for step in range(1, others)
    ]
    total = gathered(0, scatters[0])
    if levels > 2:
        lifts.append(lift(1, product(split(total), (blocks[1], None))))
    spreads[0] = spread(0, total)

    inverse_parts = [
        split(inverse) for inverse in join_inverses(inverses, triangle_parts, rows, columns)
    ]
    ratio_sums = [
        product(triangle_parts[level], inverse_parts[level + 1]) for level in range(levels)
    ]
    ratio = [split(value) for value in ratio_sums]

    for copy in fars:
        copy.wait_recv()
    full_ref[levels - 1, mine, :] = add_all([far_ref[step] for step in range(others)])
    joins = [
        send(
            full_ref.at[levels - 1, mine], full_ref.at[levels - 1, mine],
            join_send.at[step - 1], join_recv.at[step - 1], team_place(step)[1],
        )
        for step in range(1, team)
    ]
    for level in range(1, levels - 1):
        for copy in lifts[level - 1]:
            copy.wait_recv()
        terms = [lift_ref[level - 1]]
        terms += [land_ref[level - 1, step] for step in range(fanins[level] - 1)]
        total = add_all(terms)
        if level + 1 < levels - 1:
            lifts.append(lift(level + 1, product(split(total), (blocks[level + 1], None))))
        spreads[level] = spread(level, total)

    top = product(triangle_parts[levels], split(root_ref[...]), True)
    weight = []
    for level in range(levels):
        through = path[level][0].astype(F32)
        if path[level][1] is not None:
            through = through + path[level][1].astype(F32)
        carried = ratio_sums[level]
        if level < levels - 1:
            carried = product(ratio[level], path[level + 1])
        weight.append(split(carried - through))

    def known_term(level):
        for copy in spreads[level - 1]:
            copy.wait_recv()
        return product(weight[level], split(full_ref[level - 1]))

    known = [product(weight[0], leaf_parts), known_term(1)] + [None] * (levels - 2)
    cot = product(split(g_ref[...]), split(product(inverse_parts[0], path[0])), True)
    row_parts = split(q_ref[...])

    for copies in scatters + lifts + [shares, fars, joins]:
        for copy in copies:
            copy.wait_send()
    for copy in joins:
        copy.wait_recv()
    middle = top - full_ref[levels - 1]
    for level in reversed(range(levels)):
        if known[level] is None:
            known[level] = known_term(level)
        mirrored = split(mirror_lower(middle, rows, columns))
        turned = product(mirrored, (blocks[level], None), True)
        middle = known[level] + product(ratio[level], split(turned))
    mirrored = split(mirror_lower(middle, rows, columns))
    solved = split(product(mirrored, inverse_parts[0], True))
    out_ref[...] = cot + product(row_parts, solved)

    for copies in spreads:
        for copy in copies:
            copy.wait_send()


def on_device(n_outer, n_inner, leaf_q, q_cot, leaf_tri, node_blocks, node_tri, root_cot):
    fanins = fan_list(n_outer, n_inner)
    levels = len(fanins)
    order = leaf_tri.shape[1]
    groups, merged = [fanins[0]], 1
    lifted = max(levels - 2, 1)
    widest = max(fanins[1:-1] + [2]) - 1
    team = n_outer * min(2, n_inner)
    others = n_inner // min(2, n_inner)
    near = groups[-1] - 1
    dma = pltpu.SemaphoreType.DMA
    args = (leaf_q, q_cot, leaf_tri, node_blocks, node_tri, root_cot)
    return pl.pallas_call(
        functools.partial(kernel, n_outer, n_inner),
        out_shape=jax.ShapeDtypeStruct(leaf_q.shape, F32),
        in_specs=[pl.BlockSpec(memory_space=pltpu.HBM)] * len(args),
        out_specs=pl.BlockSpec(memory_space=pltpu.VMEM),
        scratch_shapes=[pltpu.VMEM(arg.shape, arg.dtype) for arg in args]
        + [
            pltpu.VMEM((merged, order, order), F32),
            pltpu.VMEM((merged, near, order // groups[0], order), F32),
            pltpu.VMEM((lifted, order // groups[-1], order), F32),
            pltpu.VMEM((lifted, widest, order // groups[-1], order), F32),
            pltpu.VMEM((levels, order, order), F32),
            pltpu.VMEM((order, order), F32),
            pltpu.VMEM((others, order // team, order), F32),
            pltpu.VMEM((team - 1, order // team, order), F32),
            dma((len(args),)),
            dma((team - 1,)),
            dma((team - 1,)),
            dma((max(others - 1, 1),)),
            dma((max(others - 1, 1),)),
            dma((team - 1,)),
            dma((team - 1,)),
            dma((merged, near)),
            dma((merged, near)),
            dma((lifted, widest)),
            dma((lifted, widest)),
            dma((levels, near)),
            dma((levels, near)),
        ],
        compiler_params=pltpu.CompilerParams(
            collective_id=0, has_side_effects=True, vmem_limit_bytes=32 * 2**20
        ),
    )(*[pltpu.with_memory_space_constraint(arg, pltpu.HBM) for arg in args])


def solution(mesh):
    return jax.shard_map(
        functools.partial(on_device, mesh.shape["outer"], mesh.shape["inner"]),
        mesh=mesh,
        in_specs=(
            P(("outer", "inner"), None),
            P(("outer", "inner"), None),
            P(("outer", "inner"), None),
            P(None, ("outer", "inner"), None),
            P(None, ("outer", "inner"), None),
            P(),
        ),
        out_specs=P(("outer", "inner"), None),
        check_vma=False,
    )
```

```python
import functools

import jax
import jax.numpy as jnp
from jax import lax
from jax.experimental import pallas as pl
from jax.experimental.pallas import tpu as pltpu
from jax.sharding import PartitionSpec as P

BLOCK = 32
MESH = pl.DeviceIdType.MESH
F32 = jnp.float32
BF16 = jnp.bfloat16


def split(value):
    high = value.astype(BF16)
    return high, (value - high.astype(F32)).astype(BF16)


def product(left, right, turn_right=False):
    left_high, left_low = left
    right_high, right_low = right
    width = right_high.shape[0 if turn_right else 1]
    along, across = (1, 0) if turn_right else (0, 1)
    wide = right_high
    if right_low is not None:
        wide = jnp.concatenate([right_high, right_low], axis=across)
    if left_low is not None:
        wide = jnp.concatenate([wide, wide], axis=along)
        left_high = jnp.concatenate([left_high, left_low], axis=1)
    total = lax.dot_general(
        left_high, wide, (((1,), (along,)), ((), ())), preferred_element_type=F32
    )
    if right_low is not None:
        total = total[:, :width] + total[:, width:]
    return total


def places(order):
    rows = lax.broadcasted_iota(jnp.int32, (order, order), 0)
    columns = lax.broadcasted_iota(jnp.int32, (order, order), 1)
    return rows, columns


def mirror_lower(matrix, rows, columns):
    below = jnp.where(rows > columns, matrix, 0.0)
    return jnp.where(rows >= columns, matrix, 0.0) + below.T


def unpack(parts, inside):
    copies = inside.shape[0] // parts[0].shape[0]
    return tuple(jnp.concatenate([part] * copies, axis=0) * inside for part in parts)


def fold(matrix, span):
    total = matrix[:span]
    for start in range(span, matrix.shape[0], span):
        total = total + matrix[start : start + span]
    return total


def block_inverses(triangles, rows, columns):
    same = rows // BLOCK == columns // BLOCK
    inside = jnp.where(same, 1.0, 0.0).astype(BF16)
    on_diagonal = rows == columns
    eye = fold(jnp.where(on_diagonal, 1.0, 0.0), BLOCK)
    stacks, scales = [], []
    for triangle in triangles:
        diagonal = jnp.where(on_diagonal, triangle, 0.0)
        down = jnp.sum(diagonal, axis=1, keepdims=True)
        scales.append(jnp.sum(diagonal, axis=0, keepdims=True))
        nilpotent = fold(jnp.where(same & (rows < columns), -triangle, 0.0) / down, BLOCK)
        stacks.append((nilpotent, eye + nilpotent))
    power = 2
    while power < BLOCK:
        following = []
        for nilpotent, total in stacks:
            parts = split(nilpotent)
            if power == 2:
                following.append((product(parts, unpack(parts, inside)), total))
                continue
            stacked = split(jnp.concatenate([nilpotent, total], axis=0))
            both = product(stacked, unpack(parts, inside))
            following.append((both[:BLOCK], total + both[BLOCK:]))
        stacks = following
        power = power * 2
    return [
        (total + product(split(total), unpack(split(nilpotent), inside))) / scale
        for (nilpotent, total), scale in zip(stacks, scales)
    ]


def join_inverses(inverses, triangle_parts, rows, columns):
    order = rows.shape[0]
    span = BLOCK
    while span < order:
        row_block, column_block = rows // span, columns // span
        corner = (rows // (2 * span) == columns // (2 * span)) & (row_block < column_block)
        corner = jnp.where(corner, 1.0, 0.0).astype(BF16)
        inside = jnp.where(row_block == column_block, 1.0, 0.0).astype(BF16)
        even = lax.rem(column_block[:span], 2) == 0
        joined = []
        for inverse, (high, low) in zip(inverses, triangle_parts):
            edge = (high * corner, None if low is None else low * corner)
            upper = split(jnp.where(even, inverse, 0.0))
            link = product(split(product(upper, edge)), unpack(split(inverse), inside))
            top = jnp.where(even, inverse, -link)
            joined.append(jnp.concatenate([top, jnp.where(even, 0.0, inverse)], axis=0))
        inverses = joined
        span = span * 2
    return inverses


def fan_list(n_outer, n_inner):
    fanins = []
    remain = n_inner
    while remain > 1:
        fanins.append(min(remain, 4))
        remain = remain // fanins[-1]
    fanins.append(n_outer)
    return fanins


def add_all(terms):
    while len(terms) > 1:
        pairs = [left + right for left, right in zip(terms[::2], terms[1::2])]
        terms = pairs + terms[len(terms) & ~1 :]
    return terms[0]


def kernel(
    n_outer, n_inner,
    q_hbm, g_hbm, leaf_hbm, blocks_hbm, tri_hbm, root_hbm, out_ref,
    q_ref, g_ref, leaf_ref, blocks_ref, tri_ref, root_ref,
    part_ref, scatter_ref, lift_ref, land_ref, full_ref,
    top_ref, far_ref, reach_ref,
    in_sem, top_send, top_recv, far_send, far_recv, join_send, join_recv,
    scatter_send, scatter_recv, lift_send, lift_recv, full_send, full_recv,
):
    fanins = fan_list(n_outer, n_inner)
    levels = len(fanins)
    groups, merged = [fanins[0]], 1
    outer, inner = lax.axis_index("outer"), lax.axis_index("inner")
    order = leaf_ref.shape[1]

    def near(size, step):
        mine = lax.rem(inner, size)
        other = lax.rem(mine + step, size)
        return other, (outer, inner + other - mine)

    def above(level, step):
        if level == levels - 1:
            return (lax.rem(outer + step, n_outer), inner)
        stride = 1
        for factor in fanins[:level]:
            stride = stride * factor
        mine = lax.rem(inner // stride, fanins[level])
        other = lax.rem(mine + step, fanins[level])
        return (outer, inner + (other - mine) * stride)

    beside = min(2, n_inner)
    team = n_outer * beside
    team_rows = order // team
    others = n_inner // beside

    def team_place(step):
        mine = outer * beside + lax.rem(inner, beside)
        other = lax.rem(mine + step, team)
        return other, (other // beside, inner - lax.rem(inner, beside) + lax.rem(other, beside))

    def far_device(step):
        return (outer, lax.rem(inner + beside * step, n_inner))

    def team_slice(place):
        return pl.ds(pl.multiple_of(place * team_rows, team_rows), team_rows)

    def own_rows(size):
        rows_each = order // size
        return pl.ds(pl.multiple_of(lax.rem(inner, size) * rows_each, rows_each), rows_each)

    loads = [
        pltpu.make_async_copy(source, target, in_sem.at[k])
        for k, (source, target) in enumerate(
            [
                (blocks_hbm, blocks_ref), (g_hbm, g_ref), (q_hbm, q_ref),
                (leaf_hbm, leaf_ref), (tri_hbm, tri_ref), (root_hbm, root_ref),
            ]
        )
    ]
    for load in loads:
        load.start()
    barrier = pltpu.get_barrier_semaphore()
    greeted = [near(groups[-1], step)[1] for step in range(1, groups[-1])]
    for level in range(merged, levels - 1):
        greeted += [above(level, step) for step in range(1, fanins[level])]
    greeted += [team_place(step)[1] for step in range(1, team)]
    greeted += [far_device(step) for step in range(1, others)]
    for device in greeted:
        pl.semaphore_signal(barrier, inc=1, device_id=device, device_id_type=MESH)

    def send(source, target, send_sem, recv_sem, device):
        copy = pltpu.make_async_remote_copy(
            src_ref=source, dst_ref=target, send_sem=send_sem, recv_sem=recv_sem,
            device_id=device, device_id_type=MESH,
        )
        copy.start()
        return copy

    def scatter(level):
        size = groups[level]
        rows_each = order // size
        copies = []
        for step in range(1, size):
            other, device = near(size, step)
            copies.append(
                send(
                    part_ref.at[level, pl.ds(pl.multiple_of(other * rows_each, rows_each), rows_each)],
                    scatter_ref.at[level, step - 1, pl.ds(0, rows_each)],
                    scatter_send.at[level, step - 1], scatter_recv.at[level, step - 1], device,
                )
            )
        return copies

    def gathered(level, copies):
        size = groups[level]
        for copy in copies:
            copy.wait_recv()
        terms = [part_ref[level, own_rows(size), :]]
        terms += [scatter_ref[level, step, : order // size] for step in range(size - 1)]
        return add_all(terms)

    def lift(level, value):
        slot = level - merged
        lift_ref[slot] = value
        return [
            send(
                lift_ref.at[slot], land_ref.at[slot, step - 1],
                lift_send.at[slot, step - 1], lift_recv.at[slot, step - 1], above(level, step),
            )
            for step in range(1, fanins[level])
        ]

    def spread(level, value):
        size = groups[min(level, merged - 1)]
        own = own_rows(size)
        full_ref[level, own, :] = value
        return [
            send(
                full_ref.at[level, own], full_ref.at[level, own],
                full_send.at[level, step - 1], full_recv.at[level, step - 1], near(size, step)[1],
            )
            for step in range(1, size)
        ]

    rows, columns = places(order)
    loads[0].wait()
    blocks = [blocks_ref[level] for level in range(levels)]
    path = [None] * levels
    path[levels - 1] = (blocks[levels - 1], None)
    for level in reversed(range(levels - 1)):
        path[level] = split(product((blocks[level], None), path[level + 1]))
    for load in loads[1:3]:
        load.wait()
    leaf_sum = product(split(g_ref[...].T), split(q_ref[...]))
    leaf_parts = split(leaf_sum)
    top_ref[...] = product(leaf_parts, path[0])
    pl.semaphore_wait(barrier, len(greeted))
    shares = []
    for step in range(1, team):
        other, device = team_place(step)
        shares.append(
            send(
                top_ref.at[team_slice(other)], reach_ref.at[step - 1],
                top_send.at[step - 1], top_recv.at[step - 1], device,
            )
        )
    part_ref[0] = product(leaf_parts, (blocks[0], None))
    scatters = [scatter(0)]

    for load in loads[3:]:
        load.wait()
    triangles = [leaf_ref[...]] + [tri_ref[level].astype(F32) for level in range(levels)]
    triangle_parts = [split(triangles[0])] + [(tri_ref[level], None) for level in range(levels)]
    inverses = block_inverses(triangles, rows, columns)

    lifts, spreads = [], [None] * (levels - 1)
    mine = team_slice(team_place(0)[0])
    for copy in shares:
        copy.wait_recv()
    far_ref[0] = add_all([top_ref[mine, :]] + [reach_ref[step] for step in range(team - 1)])
    fars = [
        send(
            far_ref.at[0], far_ref.at[step],
            far_send.at[step - 1], far_recv.at[step - 1], far_device(step),
        )
        for step in range(1, others)
    ]
    total = gathered(0, scatters[0])
    if levels > 2:
        lifts.append(lift(1, product(split(total), (blocks[1], None))))
    spreads[0] = spread(0, total)

    inverse_parts = [
        split(inverse) for inverse in join_inverses(inverses, triangle_parts, rows, columns)
    ]
    ratio_sums = [
        product(triangle_parts[level], inverse_parts[level + 1]) for level in range(levels)
    ]
    ratio = [split(value) for value in ratio_sums]

    for copy in fars:
        copy.wait_recv()
    full_ref[levels - 1, mine, :] = add_all([far_ref[step] for step in range(others)])
    joins = [
        send(
            full_ref.at[levels - 1, mine], full_ref.at[levels - 1, mine],
            join_send.at[step - 1], join_recv.at[step - 1], team_place(step)[1],
        )
        for step in range(1, team)
    ]
    for level in range(1, levels - 1):
        for copy in lifts[level - 1]:
            copy.wait_recv()
        terms = [lift_ref[level - 1]]
        terms += [land_ref[level - 1, step] for step in range(fanins[level] - 1)]
        total = add_all(terms)
        if level + 1 < levels - 1:
            lifts.append(lift(level + 1, product(split(total), (blocks[level + 1], None))))
        spreads[level] = spread(level, total)

    top = product(triangle_parts[levels], split(root_ref[...]), True)
    weight = []
    for level in range(levels):
        through = path[level][0].astype(F32)
        if path[level][1] is not None:
            through = through + path[level][1].astype(F32)
        carried = ratio_sums[level]
        if level < levels - 1:
            carried = product(ratio[level], path[level + 1])
        weight.append(split(carried - through))

    def known_term(level):
        for copy in spreads[level - 1]:
            copy.wait_recv()
        return product(weight[level], split(full_ref[level - 1]))

    known = [product(weight[0], leaf_parts), known_term(1)] + [None] * (levels - 2)
    cot = product(split(g_ref[...]), split(product(inverse_parts[0], path[0])), True)
    row_parts = split(q_ref[...])

    for copies in scatters + lifts + [shares, fars, joins]:
        for copy in copies:
            copy.wait_send()
    for copy in joins:
        copy.wait_recv()
    middle = top - full_ref[levels - 1]
    for level in reversed(range(levels)):
        if known[level] is None:
            known[level] = known_term(level)
        mirrored = split(mirror_lower(middle, rows, columns))
        turned = product(mirrored, (blocks[level], None), True)
        middle = known[level] + product(ratio[level], split(turned))
    mirrored = split(mirror_lower(middle, rows, columns))
    solved = split(product(mirrored, inverse_parts[0], True))
    out_ref[...] = cot + product(row_parts, solved)

    for copies in spreads:
        for copy in copies:
            copy.wait_send()


def on_device(n_outer, n_inner, leaf_q, q_cot, leaf_tri, node_blocks, node_tri, root_cot):
    fanins = fan_list(n_outer, n_inner)
    levels = len(fanins)
    order = leaf_tri.shape[1]
    groups, merged = [fanins[0]], 1
    lifted = max(levels - 2, 1)
    widest = max(fanins[1:-1] + [2]) - 1
    team = n_outer * min(2, n_inner)
    others = n_inner // min(2, n_inner)
    near = groups[-1] - 1
    dma = pltpu.SemaphoreType.DMA
    args = (leaf_q, q_cot, leaf_tri, node_blocks, node_tri, root_cot)
    return pl.pallas_call(
        functools.partial(kernel, n_outer, n_inner),
        out_shape=jax.ShapeDtypeStruct(leaf_q.shape, F32),
        in_specs=[pl.BlockSpec(memory_space=pltpu.HBM)] * len(args),
        out_specs=pl.BlockSpec(memory_space=pltpu.VMEM),
        scratch_shapes=[pltpu.VMEM(arg.shape, arg.dtype) for arg in args]
        + [
            pltpu.VMEM((merged, order, order), F32),
            pltpu.VMEM((merged, near, order // groups[0], order), F32),
            pltpu.VMEM((lifted, order // groups[-1], order), F32),
            pltpu.VMEM((lifted, widest, order // groups[-1], order), F32),
            pltpu.VMEM((levels, order, order), F32),
            pltpu.VMEM((order, order), F32),
            pltpu.VMEM((others, order // team, order), F32),
            pltpu.VMEM((team - 1, order // team, order), F32),
            dma((len(args),)),
            dma((team - 1,)),
            dma((team - 1,)),
            dma((max(others - 1, 1),)),
            dma((max(others - 1, 1),)),
            dma((team - 1,)),
            dma((team - 1,)),
            dma((merged, near)),
            dma((merged, near)),
            dma((lifted, widest)),
            dma((lifted, widest)),
            dma((levels, near)),
            dma((levels, near)),
        ],
        compiler_params=pltpu.CompilerParams(
            collective_id=0, has_side_effects=True, vmem_limit_bytes=32 * 2**20
        ),
    )(*[pltpu.with_memory_space_constraint(arg, pltpu.HBM) for arg in args])


def solution(mesh):
    return jax.shard_map(
        functools.partial(on_device, mesh.shape["outer"], mesh.shape["inner"]),
        mesh=mesh,
        in_specs=(
            P(("outer", "inner"), None),
            P(("outer", "inner"), None),
            P(("outer", "inner"), None),
            P(None, ("outer", "inner"), None),
            P(None, ("outer", "inner"), None),
            P(),
        ),
        out_specs=P(("outer", "inner"), None),
        check_vma=False,
    )
```
